32 devices in a mesh: expert: 8 (over z, x), dp: 4 (over y, core).
Axes of the slice: x: 2, y: 2, z: 4, core: 2. Of those that a mesh axis runs over, the one named last changes fastest.
Arguments:
- tokens: bfloat16 [16384, 4096], P(('expert', 'dp')), may hold values from -6 to 6
- out_grad: bfloat16 [16384, 4096], P(('expert', 'dp')), may hold values from -6 to 6
- gates: bfloat16 [32, 1, 24], P(('expert', 'dp')), may hold values from 0.049804688 to 1
- picks: int32 [32, 1, 24], P(('expert', 'dp')), may hold values from 0 to 511, as said below
- counts: int32 [32, 1], P(('expert', 'dp')), may hold values from 1 to 24, as said below
- w_in: bfloat16 [8, 4096, 1024], P('expert'), may hold values from -0.09375 to 0.09375
- w_out: bfloat16 [8, 4096, 1024], P('expert'), may hold values from -0.0625 to 0.0625
Outputs:
- tokens_grad: bfloat16 [16384, 4096], P(('expert', 'dp'))
- gates_grad: float32 [32, 1, 24], P(('expert', 'dp'))
- w_in_grad: bfloat16 [8, 4096, 1024], P('expert', 'dp')
- w_out_grad: bfloat16 [8, 4096, 1024], P('expert', 'dp')
The draws below stay inside these ranges and needn't reach their ends.
Inputs may be any that keep to these rules, and one draw needn't show every extreme that they name: picks[j, k, :] are 24 distinct rows of device j's tokens; slots at and beyond counts[j, k] hold rows too, but are not live. `counts`: in every draw some device fills all 24 slots of some expert.
All inputs are finite; a program needn't handle non-finite values.
Results may differ from the reference program's by a relative error of at most 0.013.
Values may be sent and summed in bfloat16 or wider, within the bound.
A program may use at most 192 MiB of HBM per device.

```python
import math
import jax
import jax.numpy as jnp
from jax import lax

D = 4096
FF = 8192
T_DEV = 512
CAP = 24
SPLIT = 8
EXPERTS = 1
FFP = 1024
TOKENS = 16384
N_EXPERT = 8
N_DP = 4
DEVICES = 32


def draw_picks(key, part):
    key = jax.random.fold_in(key, 11)
    key_list = jax.random.split(key, DEVICES * EXPERTS)

    def one_list(single_key):
        return jax.random.permutation(single_key, T_DEV)[:CAP]
    chosen = jax.vmap(one_list)(key_list)
    return chosen.reshape(DEVICES, EXPERTS, CAP).astype(jnp.int32)


def draw_counts(key, part):
    key = jax.random.fold_in(key, 23)
    first_key, second_key = jax.random.split(key)
    base_counts = jax.random.randint(first_key, (DEVICES * EXPERTS,), 1, CAP + 1)
    full_place = jax.random.randint(second_key, (), 0, DEVICES * EXPERTS)
    filled = jnp.where(jnp.arange(DEVICES * EXPERTS) == full_place, CAP, base_counts)
    return filled.reshape(DEVICES, EXPERTS).astype(jnp.int32)


def level_of(rng, dims, cuts, low, top_value):
    def one(position, blocks):
        draws = jax.random.uniform(jax.random.fold_in(jax.random.fold_in(rng, 6), position), (blocks,), jnp.float32, low / len(cuts), top_value / len(cuts))
        return jnp.repeat(jnp.exp(draws), dims[position] // blocks).reshape((-1,) + (1,) * (len(dims) - position - 1))

    gain = one(*cuts[0])
    for cut in cuts[1:]:
        gain = gain * one(*cut)
    return gain


def normal_values(own_key, dims, scale, bound, cuts=(), kind=jnp.bfloat16):
    drawn = scale * jax.random.normal(own_key, dims, jnp.float32)
    if cuts:
        drawn = drawn * level_of(own_key, dims, cuts, -0.22, 0.18)
    return jnp.clip(drawn, -bound, bound).astype(kind)


def setup_inputs(seed: int = 0) -> dict:
    keys = jax.random.split(jax.random.key(seed), 8)
    tokens = normal_values(keys[0], (TOKENS, D), 1.0, 6.0, ((0, 32),))
    out_grad = normal_values(keys[1], (TOKENS, D), 1.0, 6.0, ((0, 32),))
    gates = jnp.clip(jnp.exp(math.log(1.0) - 2.9996462 * jax.random.uniform(keys[2], (DEVICES, EXPERTS, CAP), jnp.float32) ** level_of(keys[2], (DEVICES, EXPERTS, CAP), ((0, 32),), -0.2, 0.2)), 0.049804688, 1.0).astype(jnp.bfloat16)
    picks = draw_picks(jax.random.fold_in(keys[7], 71), 0)
    counts = draw_counts(jax.random.fold_in(keys[7], 71), 0)
    w_in = normal_values(keys[5], (N_EXPERT, D, FFP), D ** -0.5, 0.09375, ((0, 8),))
    w_out = normal_values(keys[6], (N_EXPERT, D, FFP), FF ** -0.5, 0.0625, ((0, 8),))
    return dict(tokens=tokens, out_grad=out_grad, gates=gates, picks=picks, counts=counts, w_in=w_in, w_out=w_out)


def take_rows(table, index_rows):
    return table[index_rows]

def add_rows(buffer, index_rows, values):
    return buffer.at[index_rows].add(values)

def reference(tokens, out_grad, gates, picks, counts, w_in, w_out):
    device_count = N_EXPERT * N_DP
    token_table = tokens.reshape(device_count, T_DEV, D)
    grad_table = out_grad.reshape(device_count, T_DEV, D)
    flat_picks = picks.reshape(device_count, EXPERTS * CAP)
    picked_x = jax.vmap(take_rows)(token_table, flat_picks).reshape(device_count, EXPERTS, CAP, D)
    picked_dy = jax.vmap(take_rows)(grad_table, flat_picks).reshape(device_count, EXPERTS, CAP, D)
    live = jnp.arange(CAP)[None, None, :] < counts[:, :, None]
    scale = jnp.where(live, gates, jnp.zeros_like(gates))
    scaled_dy = (scale.astype(jnp.float32)[..., None] * picked_dy.astype(jnp.float32)).astype(jnp.bfloat16)
    whole_in = w_in.reshape(EXPERTS, SPLIT, D, FFP).transpose(0, 2, 1, 3).reshape(EXPERTS, D, FF)
    whole_out = w_out.reshape(EXPERTS, SPLIT, D, FFP).transpose(0, 2, 1, 3).reshape(EXPERTS, D, FF)
    row_grads = []
    gate_grads = []
    in_grads = []
    out_grads = []
    for expert_k in range(EXPERTS):
        rows_x = picked_x[:, expert_k].reshape(-1, D)
        rows_dy = picked_dy[:, expert_k].reshape(-1, D)
        rows_scaled = scaled_dy[:, expert_k].reshape(-1, D)
        pre = jnp.dot(rows_x, whole_in[expert_k], preferred_element_type=jnp.float32)
        hidden, gelu_back = jax.vjp(jax.nn.gelu, pre)
        hidden = hidden.astype(jnp.bfloat16)
        expert_out = lax.dot_general(hidden, whole_out[expert_k], (((1,), (1,)), ((), ())), preferred_element_type=jnp.float32)
        gate_grads.append(lax.optimization_barrier(jnp.sum(rows_dy.astype(jnp.float32) * expert_out, axis=-1)).reshape(device_count, CAP))
        hidden_grad = jnp.dot(rows_scaled, whole_out[expert_k], preferred_element_type=jnp.float32)
        pre_grad = gelu_back(hidden_grad)[0].astype(jnp.bfloat16)
        row_grad = lax.dot_general(pre_grad, whole_in[expert_k], (((1,), (1,)), ((), ())), preferred_element_type=jnp.float32)
        row_grads.append(row_grad.reshape(device_count, CAP, D))
        group_x = rows_x.reshape(N_EXPERT, N_DP, CAP, D)
        group_dy = rows_scaled.reshape(N_EXPERT, N_DP, CAP, D)
        group_pre = pre_grad.reshape(N_EXPERT, N_DP, CAP, FF)
        group_hidden = hidden.reshape(N_EXPERT, N_DP, CAP, FF)
        in_total = jnp.zeros((D, FF), jnp.float32)
        out_total = jnp.zeros((D, FF), jnp.float32)
        for batch_d in range(N_DP):
            x_rows = group_x[:, batch_d].reshape(-1, D)
            dy_rows = group_dy[:, batch_d].reshape(-1, D)
            term_in = jnp.dot(x_rows.T, group_pre[:, batch_d].reshape(-1, FF), preferred_element_type=jnp.float32)
            term_out = jnp.dot(dy_rows.T, group_hidden[:, batch_d].reshape(-1, FF), preferred_element_type=jnp.float32)
            term_in = lax.optimization_barrier(term_in.astype(jnp.bfloat16))
            term_out = lax.optimization_barrier(term_out.astype(jnp.bfloat16))
            in_total = in_total + term_in.astype(jnp.float32)
            out_total = out_total + term_out.astype(jnp.float32)
        in_grads.append(in_total.astype(jnp.bfloat16).reshape(D, SPLIT, FFP).transpose(1, 0, 2))
        out_grads.append(out_total.astype(jnp.bfloat16).reshape(D, SPLIT, FFP).transpose(1, 0, 2))
    all_rows = jnp.stack(row_grads, axis=1).reshape(device_count, EXPERTS * CAP, D)
    empty = jnp.zeros((device_count, T_DEV, D), jnp.float32)
    tokens_grad = jax.vmap(add_rows)(empty, flat_picks, all_rows).reshape(T_DEV * device_count, D).astype(jnp.bfloat16)
    gate_all = jnp.stack(gate_grads, axis=1)
    gates_grad = jnp.where(live, gate_all, jnp.zeros_like(gate_all))
    w_in_grad = jnp.concatenate(in_grads, axis=0)
    w_out_grad = jnp.concatenate(out_grads, axis=0)
    return (tokens_grad, gates_grad, w_in_grad, w_out_grad)
```

```python
import functools

import jax
import jax.numpy as jnp
from jax import lax
from jax.experimental import pallas as pl
from jax.experimental.pallas import tpu as pltpu
from jax.sharding import PartitionSpec as P

FF = 8192
LANES = 128
MESH = pl.DeviceIdType.MESH


def meet(peers):
    barrier = pltpu.get_barrier_semaphore()
    for peer in peers:
        pl.semaphore_signal(barrier, inc=1, device_id=peer, device_id_type=MESH)
    pl.semaphore_wait(barrier, len(peers))


def send(src, dst, send_sem, recv_sem, peer):
    copy = pltpu.make_async_remote_copy(
        src_ref=src,
        dst_ref=dst,
        send_sem=send_sem,
        recv_sem=recv_sem,
        device_id=peer,
        device_id_type=MESH,
    )
    copy.start()
    return copy


def gather_kernel(
    width,
    own_x,
    own_dy,
    rows,
    slices,
    own_sem,
    z_send,
    z_recv,
    x_send,
    x_recv,
    dp_send,
    dp_recv,
    keep_sem,
):
    count = rows.shape[1]
    parts = slices.shape[1]
    lines = count // 2
    e = lax.axis_index("expert")
    d = lax.axis_index("dp")
    after = lax.rem(e + 2, count)
    before = lax.rem(e + count - 2, count)
    beside = e + 1 - 2 * lax.rem(e, 2)
    own = (
        pltpu.make_async_copy(own_x, rows.at[0, e], own_sem.at[0]),
        pltpu.make_async_copy(own_dy, rows.at[1, e], own_sem.at[1]),
    )
    for copy in own:
        copy.start()
    meet(
        [(after, d), (before, d), (beside, d)]
        + [(e, lax.rem(d + k, parts)) for k in range(1, parts)]
    )
    for copy in own:
        copy.wait()

    sent = []

    def block(b, c):
        return rows.at[:, b, :, pl.ds(c * width, width)]

    def to_z(b, s, c):
        sent.append(send(block(b, c), block(b, c), z_send.at[s, c], z_recv.at[s, c], (after, d)))

    def to_x(b, s, c):
        sent.append(send(block(b, c), block(b, c), x_send.at[s, c], x_recv.at[s, c], (beside, d)))

    def to_dp(b, c):
        @pl.when(d == c)
        def _():
            pltpu.make_async_copy(block(b, c), slices.at[:, d, b], keep_sem).start()

        @pl.when(d != c)
        def _():
            send(block(b, c), slices.at[:, d, b], dp_send, dp_recv.at[d], (e, c))

    def arrived(b, c, sem):
        pltpu.make_async_copy(block(b, c), block(b, c), sem).wait()

    for s in range(lines + 1):
        if s < lines:
            b = lax.rem(e + count - 2 * s, count)
            for c in range(parts):
                if s > 0:
                    arrived(b, c, z_recv.at[s - 1, c])
                if s < lines - 1:
                    to_z(b, s, c)
                to_x(b, s, c)
                to_dp(b, c)
        if s > 0:
            b = lax.rem(beside + count - 2 * (s - 1), count)
            for c in range(parts):
                arrived(b, c, x_recv.at[s - 1, c])
                to_dp(b, c)
    for copy in sent:
        copy.wait_send()
    out = slices.at[:, pl.ds(0, parts - 1)]
    pltpu.make_async_copy(out, out, dp_send).wait()
    kept = slices.at[:, d]
    pltpu.make_async_copy(kept, kept, keep_sem).wait()
    for k in range(1, parts):
        came = slices.at[:, lax.rem(d + k, parts)]
        pltpu.make_async_copy(came, came, dp_recv.at[lax.rem(d + k, parts)]).wait()


def gather_rows(own_x, own_dy, count, parts):
    slots, model_width = own_x.shape
    width = model_width // parts
    lines = count // 2
    dma = pltpu.SemaphoreType.DMA
    return pl.pallas_call(
        functools.partial(gather_kernel, width),
        out_shape=(
            jax.ShapeDtypeStruct((2, count, slots, model_width), jnp.bfloat16),
            jax.ShapeDtypeStruct((2, parts, count, slots, width), jnp.bfloat16),
        ),
        in_specs=[pl.BlockSpec(memory_space=pl.ANY)] * 2,
        out_specs=[pl.BlockSpec(memory_space=pl.ANY)] * 2,
        scratch_shapes=[
            dma((2,)),
            dma((lines - 1, parts)),
            dma((lines - 1, parts)),
            dma((lines, parts)),
            dma((lines, parts)),
            dma,
            dma((parts,)),
            dma,
        ],
        compiler_params=pltpu.CompilerParams(collective_id=0, has_side_effects=True),
        cost_estimate=pl.CostEstimate(flops=0, bytes_accessed=12 << 20, transcendentals=0),
        name="gather_rows",
    )(own_x, own_dy)


def return_kernel(
    spans,
    pre_grad,
    hidden,
    gate,
    weight,
    all_pre,
    all_hidden,
    rows_out,
    gates_out,
    w1,
    terms,
    beside_terms,
    pair_sum,
    line_terms,
    w_sem,
    own_sem,
    a_send,
    a_recv,
    x_send,
    x_recv,
    z_send,
    z_recv,
):
    parts = all_pre.shape[0]
    lines, slots = pair_sum.shape[0], pair_sum.shape[1]
    count = 2 * lines
    model_width = rows_out.shape[1]
    e = lax.axis_index("expert")
    d = lax.axis_index("dp")
    z = e // 2
    x = lax.rem(e, 2)
    beside = e + 1 - 2 * x
    twin = d + 1 - 2 * lax.rem(d, 2)
    across = lax.rem(d + 2, parts)
    load = pltpu.make_async_copy(weight, w1, w_sem)
    load.start()
    meet(
        [(beside, d), (e, twin), (e, across)]
        + [(lax.rem(e + 2 * t, count), d) for t in range(1, lines)]
    )
    sent = []
    pairs = ((pre_grad, all_pre), (hidden, all_hidden))
    for i, (src, dst) in enumerate(pairs):
        sent.append(send(src, dst.at[d], a_send.at[0, i], a_recv.at[0, i], (e, across)))
    for i, (src, dst) in enumerate(pairs):
        sent.append(send(src, dst.at[d], a_send.at[1, i], a_recv.at[1, i], (e, twin)))
        pltpu.make_async_copy(src, dst.at[d], own_sem.at[i]).start()

    def to_x(k):
        start, size = spans[k]
        cols = pl.ds(start, size)
        sent.append(
            send(
                terms.at[1 - x, :, :, cols],
                beside_terms.at[:, :, cols],
                x_send.at[k],
                x_recv.at[k],
                (beside, d),
            )
        )

    def keep(k, value):
        start, size = spans[k]
        value = value.reshape(lines, 2, slots, size).astype(jnp.bfloat16)
        terms[0, :, :, start : start + size] = value[:, 0]
        terms[1, :, :, start : start + size] = value[:, 1]

    keep(0, gate[...])
    to_x(0)
    load.wait()
    for k in range(1, len(spans)):
        start, size = spans[k]
        keep(
            k,
            lax.dot_general(
                pre_grad[...],
                w1[start : start + size, :],
                (((1,), (1,)), ((), ())),
                preferred_element_type=jnp.float32,
            ),
        )
        to_x(k)
    for k, (start, size) in enumerate(spans):
        cols = slice(start, start + size)
        here = pl.ds(start, size)
        pltpu.make_async_copy(
            beside_terms.at[:, :, here], beside_terms.at[:, :, here], x_recv.at[k]
        ).wait()
        pair_sum[:, :, cols] = (
            terms[x, :, :, cols].astype(jnp.float32)
            + beside_terms[:, :, cols].astype(jnp.float32)
        ).astype(jnp.bfloat16)
        for t in range(1, lines):
            sent.append(
                send(
                    pair_sum.at[lax.rem(z + t, lines), :, here],
                    line_terms.at[t - 1, :, here],
                    z_send.at[t - 1, k],
                    z_recv.at[t - 1, k],
                    (lax.rem(e + 2 * t, count), d),
                )
            )
    for i, (_, dst) in enumerate(pairs):
        came = dst.at[across]
        pltpu.make_async_copy(came, came, a_recv.at[0, i]).wait()
        sent.append(send(came, came, a_send.at[2, i], a_recv.at[2, i], (e, twin)))
    for k, (start, size) in enumerate(spans):
        cols = slice(start, start + size)
        here = pl.ds(start, size)
        total = terms[x, z, :, cols].astype(jnp.float32) + beside_terms[z, :, cols].astype(
            jnp.float32
        )
        for t in range(1, lines):
            came = line_terms.at[t - 1, :, here]
            pltpu.make_async_copy(came, came, z_recv.at[t - 1, k]).wait()
            total += line_terms[t - 1, :, cols].astype(jnp.float32)
        if start < model_width:
            rows_out[:, cols] = total.astype(jnp.bfloat16)
        else:
            gates_out[...] = total
    for i, (src, dst) in enumerate(pairs):
        pltpu.make_async_copy(src, dst.at[d], own_sem.at[i]).wait()
        for step, slot in ((1, twin), (2, lax.rem(twin + 2, parts))):
            came = dst.at[slot]
            pltpu.make_async_copy(came, came, a_recv.at[step, i]).wait()
    for copy in sent:
        copy.wait_send()


def return_rows(pre_grad, hidden, gate, weight, count, parts):
    row_count, units = pre_grad.shape
    slots = row_count // count
    lines = count // 2
    model_width = weight.shape[0]
    width = model_width // 4
    spans = [(model_width, LANES)] + [(k * width, width) for k in range(4)]
    wide = model_width + LANES
    dma = pltpu.SemaphoreType.DMA
    vmem = pl.BlockSpec(memory_space=pltpu.VMEM)
    anywhere = pl.BlockSpec(memory_space=pl.ANY)
    return pl.pallas_call(
        functools.partial(return_kernel, spans),
        out_shape=(
            jax.ShapeDtypeStruct((parts, row_count, units), jnp.bfloat16),
            jax.ShapeDtypeStruct((parts, row_count, units), jnp.bfloat16),
            jax.ShapeDtypeStruct((slots, model_width), jnp.bfloat16),
            jax.ShapeDtypeStruct((slots, LANES), jnp.float32),
        ),
        in_specs=[vmem, vmem, vmem, anywhere],
        out_specs=[anywhere, anywhere, vmem, vmem],
        scratch_shapes=[
            pltpu.VMEM((model_width, units), jnp.bfloat16),
            pltpu.VMEM((2, lines, slots, wide), jnp.bfloat16),
            pltpu.VMEM((lines, slots, wide), jnp.bfloat16),
            pltpu.VMEM((lines, slots, wide), jnp.bfloat16),
            pltpu.VMEM((lines - 1, slots, wide), jnp.bfloat16),
            dma,
            dma((2,)),
            dma((3, 2)),
            dma((3, 2)),
            dma((len(spans),)),
            dma((len(spans),)),
            dma((lines - 1, len(spans))),
            dma((lines - 1, len(spans))),
        ],
        compiler_params=pltpu.CompilerParams(
            collective_id=1, has_side_effects=True, vmem_limit_bytes=40 << 20
        ),
        cost_estimate=pl.CostEstimate(
            flops=2 * row_count * units * model_width,
            bytes_accessed=20 << 20,
            transcendentals=0,
        ),
        name="return_rows",
    )(pre_grad, hidden, gate, weight)


def local(tokens, out_grad, gates, picks, counts, w_in, w_out):
    t_dev, model_width = tokens.shape
    slot_count = picks.shape[2]
    parts = lax.axis_size("dp")
    count = lax.axis_size("expert")
    weight_in, weight_out = w_in[0], w_out[0]
    live = jnp.arange(slot_count)[None, :] < counts[0][:, None]
    scale = jnp.where(live, gates[0], jnp.zeros_like(gates[0]))
    chosen = picks[0, 0][:, None] == jnp.arange(t_dev)[None, :]
    chosen = chosen.astype(jnp.bfloat16)

    def pick(table):
        return jnp.dot(chosen, table, preferred_element_type=jnp.float32).astype(jnp.bfloat16)

    row_scale = lax.all_gather(scale[0], "expert", tiled=True).astype(jnp.float32)[:, None]
    rows, slices = gather_rows(pick(tokens), pick(out_grad), count, parts)
    row_count = count * slot_count
    pre = jnp.dot(
        rows[0].reshape(row_count, model_width), weight_in, preferred_element_type=jnp.float32
    )
    back = jnp.dot(
        rows[1].reshape(row_count, model_width), weight_out, preferred_element_type=jnp.float32
    )
    hidden, gelu_back = jax.vjp(jax.nn.gelu, pre)
    gate_part = jnp.sum(hidden * back, axis=-1, keepdims=True)
    gate_part = jnp.broadcast_to(gate_part, (row_count, LANES))
    pre_grad = gelu_back(row_scale * back)[0].astype(jnp.bfloat16)
    scaled_hidden = (row_scale * hidden).astype(jnp.bfloat16)
    all_pre, all_hidden, summed_rows, summed_gates = return_rows(
        pre_grad, scaled_hidden, gate_part, weight_in, count, parts
    )

    def weight_grad(columns, units):
        return lax.dot_general(
            columns.reshape(parts * row_count, model_width // parts),
            units.reshape(parts * row_count, units.shape[-1]),
            (((0,), (0,)), ((), ())),
            preferred_element_type=jnp.float32,
        ).astype(jnp.bfloat16)[None]

    tokens_grad = lax.dot_general(
        chosen, summed_rows, (((0,), (0,)), ((), ())), preferred_element_type=jnp.float32
    ).astype(jnp.bfloat16)
    gates_grad = jnp.where(live, summed_gates[:, 0][None], 0.0)[None]
    return (
        tokens_grad,
        gates_grad,
        weight_grad(slices[0], all_pre),
        weight_grad(slices[1], all_hidden),
    )


def local_many(tokens, out_grad, gates, picks, counts, w_in, w_out):
    t_dev, model_width = tokens.shape
    expert_count = picks.shape[1]
    slot_count = picks.shape[2]
    part_units = w_in.shape[2]
    part_count = FF // part_units
    expert_devices = lax.axis_size("expert")
    row_index = picks[0].reshape(-1)
    live = jnp.arange(slot_count)[None, :] < counts[0][:, None]
    scale = jnp.where(live, gates[0], jnp.zeros_like(gates[0]))

    def exchange(values):
        return lax.all_to_all(values, "expert", split_axis=0, concat_axis=0, tiled=True)

    def spread(values):
        wide = jnp.broadcast_to(values[:, None], (expert_count, part_count) + values.shape[1:])
        return exchange(wide.reshape((expert_devices,) + values.shape[1:]))

    row_count = expert_devices * slot_count
    picked_shape = (expert_count, slot_count, model_width)
    rows_x = spread(tokens[row_index].reshape(picked_shape)).reshape(row_count, model_width)
    rows_dy = spread(out_grad[row_index].reshape(picked_shape)).reshape(row_count, model_width)
    row_scale = spread(scale).reshape(row_count, 1).astype(jnp.float32)
    weight_in, weight_out = w_in[0], w_out[0]
    pre = jnp.dot(rows_x, weight_in, preferred_element_type=jnp.float32)
    back = jnp.dot(rows_dy, weight_out, preferred_element_type=jnp.float32)
    hidden, gelu_back = jax.vjp(jax.nn.gelu, pre)
    gate_part = jnp.sum(hidden * back, axis=-1)
    pre_grad = gelu_back(row_scale * back)[0].astype(jnp.bfloat16)
    scaled_hidden = (row_scale * hidden).astype(jnp.bfloat16)
    row_part = lax.dot_general(
        pre_grad, weight_in, (((1,), (1,)), ((), ())), preferred_element_type=jnp.float32
    )

    def weight_grad(columns, units):
        columns = lax.all_to_all(columns, "dp", split_axis=1, concat_axis=0, tiled=True)
        units = lax.all_gather(units, "dp", axis=0, tiled=True)
        return lax.dot_general(
            columns, units, (((0,), (0,)), ((), ())), preferred_element_type=jnp.float32
        ).astype(jnp.bfloat16)[None]

    back_shape = (expert_devices, slot_count, model_width)
    back_rows = exchange(row_part.reshape(back_shape).astype(jnp.bfloat16)).astype(jnp.float32)
    back_gates = exchange(gate_part.reshape(back_shape[:2]))
    summed_rows = jnp.sum(back_rows.reshape((expert_count, part_count) + back_shape[1:]), axis=1)
    summed_gates = jnp.sum(back_gates.reshape(expert_count, part_count, slot_count), axis=1)
    empty_rows = jnp.zeros((t_dev, model_width), jnp.float32)
    tokens_grad = (
        empty_rows.at[row_index].add(summed_rows.reshape(-1, model_width)).astype(jnp.bfloat16)
    )
    gates_grad = jnp.where(live, summed_gates, jnp.zeros_like(summed_gates))[None]
    return (
        tokens_grad,
        gates_grad,
        weight_grad(rows_x, pre_grad),
        weight_grad(rows_dy, scaled_hidden),
    )


def solution(mesh):
    placed = (
        P(("expert", "dp"), None),
        P(("expert", "dp"), None),
        P(("expert", "dp"), None, None),
        P(("expert", "dp"), None, None),
        P(("expert", "dp"), None),
        P("expert", None, None),
        P("expert", None, None),
    )

    def run(*arrays):
        one = arrays[3].shape[1] == 1 and mesh.shape["dp"] == 4
        return jax.shard_map(
            local if one else local_many,
            mesh=mesh,
            in_specs=placed,
            out_specs=(
                P(("expert", "dp"), None),
                P(("expert", "dp"), None, None),
                P("expert", "dp", None),
                P("expert", "dp", None),
            ),
            check_vma=False,
        )(*arrays)

    return run
```

```python
import functools

import jax
import jax.numpy as jnp
from jax import lax
from jax.experimental import pallas as pl
from jax.experimental.pallas import tpu as pltpu
from jax.sharding import PartitionSpec as P

FF = 8192
LANES = 128
ROOT = 0.7978845608028654
CUBE = 0.044715
MESH = pl.DeviceIdType.MESH


def meet(peers):
    barrier = pltpu.get_barrier_semaphore()
    for peer in peers:
        pl.semaphore_signal(barrier, inc=1, device_id=peer, device_id_type=MESH)
    pl.semaphore_wait(barrier, len(peers))


def send(src, dst, send_sem, recv_sem, peer):
    copy = pltpu.make_async_remote_copy(
        src_ref=src,
        dst_ref=dst,
        send_sem=send_sem,
        recv_sem=recv_sem,
        device_id=peer,
        device_id_type=MESH,
    )
    copy.start()
    return copy


def layer_kernel(
    spans,
    tokens,
    out_grad,
    picks,
    gates,
    counts,
    weight_in,
    weight_out,
    slices,
    all_pre,
    all_hidden,
    rows_out,
    gates_out,
    tables,
    w1,
    w2,
    rows,
    scales,
    pre,
    back,
    gate,
    pre_grad,
    hidden,
    terms,
    beside_terms,
    pair_sum,
    line_terms,
    table_sem,
    w_sem,
    s_send,
    s_recv,
    g_send,
    g_recv,
    gx_send,
    gx_recv,
    dp_send,
    dp_recv,
    keep_sem,
    own_sem,
    a_send,
    a_recv,
    x_send,
    x_recv,
    z_send,
    z_recv,
):
    parts = all_pre.shape[0]
    count, slots, model_width = rows.shape[1:]
    row_count = count * slots
    lines = count // 2
    width = model_width // parts
    e = lax.axis_index("expert")
    d = lax.axis_index("dp")
    z = e // 2
    x = lax.rem(e, 2)
    after = lax.rem(e + 2, count)
    beside = e + 1 - 2 * x
    twin = d + 1 - 2 * lax.rem(d, 2)
    across = lax.rem(d + 2, parts)
    loads = [
        pltpu.make_async_copy(src, tables.at[i], table_sem.at[i])
        for i, src in enumerate((tokens, out_grad))
    ] + [
        pltpu.make_async_copy(src, dst, w_sem.at[i])
        for i, (src, dst) in enumerate(((weight_in, w1), (weight_out, w2)))
    ]
    for copy in loads:
        copy.start()
    group = [lax.rem(e + 2 * t, count) for t in range(1, lines)]
    group += [lax.rem(beside + 2 * t, count) for t in range(lines)]
    meet([(peer, d) for peer in group] + [(e, lax.rem(d + k, parts)) for k in range(1, parts)])
    sent = []

    def block(b, c):
        return rows.at[:, b, :, pl.ds(c * width, width)]

    def to_z(b, s, c):
        sent.append(send(block(b, c), block(b, c), g_send.at[s, c], g_recv.at[s, c], (after, d)))

    def to_beside(b, s, c):
        sent.append(send(block(b, c), block(b, c), gx_send.at[s, c], gx_recv.at[s, c], (beside, d)))

    def to_dp(b, c):
        @pl.when(d == c)
        def _():
            pltpu.make_async_copy(block(b, c), slices.at[:, d, b], keep_sem).start()

        @pl.when(d != c)
        def _():
            send(block(b, c), slices.at[:, d, b], dp_send, dp_recv.at[d], (e, c))

    def arrived(ref, sem):
        pltpu.make_async_copy(ref, ref, sem).wait()

    chosen = lax.broadcasted_iota(jnp.int32, (tables.shape[1], slots), 0) == picks[...]
    chosen = chosen.astype(jnp.float32).astype(jnp.bfloat16)
    for copy in loads[:2]:
        copy.wait()
    for c in range(parts):
        cols = slice(c * width, (c + 1) * width)
        for i in range(2):
            rows[i, e, :, cols] = lax.dot_general(
                chosen,
                tables[i, :, cols],
                (((0,), (0,)), ((), ())),
                preferred_element_type=jnp.float32,
            ).astype(jnp.bfloat16)
        to_beside(e, 0, c)
        to_z(e, 0, c)
        to_dp(e, c)
    slot = lax.broadcasted_iota(jnp.int32, (slots, slots), 1)
    live = slot == lax.broadcasted_iota(jnp.int32, (slots, slots), 0)
    live = jnp.logical_and(live, slot < counts[...])
    scale = jnp.where(live, jnp.broadcast_to(gates[...].astype(jnp.float32), (slots, slots)), 0.0)
    scale = jnp.sum(scale, axis=1, keepdims=True)
    scales[e] = jnp.broadcast_to(scale, (slots, LANES))
    for i, peer in enumerate(group):
        sent.append(send(scales.at[e], scales.at[e], s_send.at[i], s_recv.at[e], (peer, d)))

    def multiply(c):
        cols = slice(c * width, (c + 1) * width)
        for i, (weight, total) in enumerate(((w1, pre), (w2, back))):
            part = rows[i, :, :, cols].astype(jnp.float32).reshape(row_count, width)
            part = jnp.dot(
                part.astype(jnp.bfloat16), weight[cols, :], preferred_element_type=jnp.float32
            )
            if c == 0:
                total[...] = part
            else:
                total[...] += part

    for s in range(1, lines + 1):
        if s < lines:
            b = lax.rem(e + count - 2 * s, count)
            for c in range(parts):
                arrived(block(b, c), g_recv.at[s - 1, c])
                to_beside(b, s, c)
                if s < lines - 1:
                    to_z(b, s, c)
                to_dp(b, c)
        b = lax.rem(beside + count - 2 * (s - 1), count)
        for c in range(parts):
            arrived(block(b, c), gx_recv.at[s - 1, c])
            to_dp(b, c)
            if s == lines:
                if c == 0:
                    for copy in loads[2:]:
                        copy.wait()
                multiply(c)

    for peer in group:
        arrived(scales.at[peer], s_recv.at[peer])
    row_scale = scales[...].reshape(row_count, LANES)
    step = 32
    for start in range(0, row_count, step):
        here = slice(start, start + step)
        v, g, scale = pre[here, :], back[here, :], row_scale[here, :1]
        square = v * v
        bend = jnp.tanh(ROOT * v * (1.0 + CUBE * square))
        half = 0.5 * (1.0 + bend)
        value = v * half
        slope = half + 0.5 * v * (1.0 - bend * bend) * ROOT * (1.0 + 3.0 * CUBE * square)
        pre_grad[here, :] = (scale * g * slope).astype(jnp.bfloat16)
        hidden[here, :] = (scale * value).astype(jnp.bfloat16)
        gate[here, :] = jnp.broadcast_to(
            jnp.sum(value * g, axis=1, keepdims=True), (step, LANES)
        )

    pairs = ((pre_grad, all_pre), (hidden, all_hidden))
    for i, (src, dst) in enumerate(pairs):
        sent.append(send(src, dst.at[d], a_send.at[0, i], a_recv.at[0, i], (e, across)))
    for i, (src, dst) in enumerate(pairs):
        sent.append(send(src, dst.at[d], a_send.at[1, i], a_recv.at[1, i], (e, twin)))
        pltpu.make_async_copy(src, dst.at[d], own_sem.at[i]).start()

    def to_x(k, value):
        start, size = spans[k]
        cols = pl.ds(start, size)
        value = value.reshape(lines, 2, slots, size).astype(jnp.bfloat16)
        terms[0, :, :, start : start + size] = value[:, 0]
        terms[1, :, :, start : start + size] = value[:, 1]
        sent.append(
            send(
                terms.at[1 - x, :, :, cols],
                beside_terms.at[:, :, cols],
                x_send.at[k],
                x_recv.at[k],
                (beside, d),
            )
        )

    def to_lines(k):
        start, size = spans[k]
        cols = slice(start, start + size)
        here = pl.ds(start, size)
        arrived(beside_terms.at[:, :, here], x_recv.at[k])
        pair_sum[:, :, cols] = (
            terms[x, :, :, cols].astype(jnp.float32)
            + beside_terms[:, :, cols].astype(jnp.float32)
        ).astype(jnp.bfloat16)
        for t in range(1, lines):
            sent.append(
                send(
                    pair_sum.at[lax.rem(z + t, lines), :, here],
                    line_terms.at[t - 1, :, here],
                    z_send.at[t - 1, k],
                    z_recv.at[t - 1, k],
                    (lax.rem(e + 2 * t, count), d),
                )
            )

    to_x(0, gate[...])
    for k in range(1, len(spans)):
        start, size = spans[k]
        to_x(
            k,
            lax.dot_general(
                pre_grad[...],
                w1[start : start + size, :],
                (((1,), (1,)), ((), ())),
                preferred_element_type=jnp.float32,
            ),
        )
    for k in range(len(spans)):
        to_lines(k)
    for i, (_, dst) in enumerate(pairs):
        arrived(dst.at[across], a_recv.at[0, i])
        sent.append(
            send(dst.at[across], dst.at[across], a_send.at[2, i], a_recv.at[2, i], (e, twin))
        )
    for k, (start, size) in enumerate(spans):
        cols = slice(start, start + size)
        total = terms[x, z, :, cols].astype(jnp.float32)
        total += beside_terms[z, :, cols].astype(jnp.float32)
        for t in range(1, lines):
            arrived(line_terms.at[t - 1, :, pl.ds(start, size)], z_recv.at[t - 1, k])
            total += line_terms[t - 1, :, cols].astype(jnp.float32)
        if start < model_width:
            rows_out[:, cols] = total.astype(jnp.bfloat16)
        else:
            gates_out[...] = total
    for i, (src, dst) in enumerate(pairs):
        pltpu.make_async_copy(src, dst.at[d], own_sem.at[i]).wait()
        for hop, owner in ((1, twin), (2, lax.rem(twin + 2, parts))):
            arrived(dst.at[owner], a_recv.at[hop, i])
    for copy in sent:
        copy.wait_send()
    arrived(slices.at[:, pl.ds(0, parts - 1)], dp_send)
    arrived(slices.at[:, d], keep_sem)
    for k in range(1, parts):
        owner = lax.rem(d + k, parts)
        arrived(slices.at[:, owner], dp_recv.at[owner])


def layer(tokens, out_grad, picks, gates, counts, weight_in, weight_out, count, parts):
    t_dev, model_width = tokens.shape
    slots = picks.shape[-1]
    units = weight_in.shape[1]
    row_count = count * slots
    lines = count // 2
    width = model_width // parts
    spans = [(model_width, LANES)] + [(k * width, width) for k in range(parts)]
    wide = model_width + LANES
    dma = pltpu.SemaphoreType.DMA
    vmem = pl.BlockSpec(memory_space=pltpu.VMEM)
    anywhere = pl.BlockSpec(memory_space=pl.ANY)
    bf16, f32 = jnp.bfloat16, jnp.float32
    return pl.pallas_call(
        functools.partial(layer_kernel, spans),
        out_shape=(
            jax.ShapeDtypeStruct((2, parts, count, slots, width), bf16),
            jax.ShapeDtypeStruct((parts, row_count, units), bf16),
            jax.ShapeDtypeStruct((parts, row_count, units), bf16),
            jax.ShapeDtypeStruct((slots, model_width), bf16),
            jax.ShapeDtypeStruct((slots, LANES), f32),
        ),
        in_specs=[anywhere, anywhere, vmem, vmem, vmem, anywhere, anywhere],
        out_specs=[anywhere, anywhere, anywhere, vmem, vmem],
        scratch_shapes=[
            pltpu.VMEM((2, t_dev, model_width), bf16),
            pltpu.VMEM((model_width, units), bf16),
            pltpu.VMEM((model_width, units), bf16),
            pltpu.VMEM((2, count, slots, model_width), bf16),
            pltpu.VMEM((count, slots, LANES), f32),
            pltpu.VMEM((row_count, units), f32),
            pltpu.VMEM((row_count, units), f32),
            pltpu.VMEM((row_count, LANES), f32),
            pltpu.VMEM((row_count, units), bf16),
            pltpu.VMEM((row_count, units), bf16),
            pltpu.VMEM((2, lines, slots, wide), bf16),
            pltpu.VMEM((lines, slots, wide), bf16),
            pltpu.VMEM((lines, slots, wide), bf16),
            pltpu.VMEM((lines - 1, slots, wide), bf16),
            dma((2,)),
            dma((2,)),
            dma((count - 1,)),
            dma((count,)),
            dma((lines - 1, parts)),
            dma((lines - 1, parts)),
            dma((lines, parts)),
            dma((lines, parts)),
            dma,
            dma((parts,)),
            dma,
            dma((2,)),
            dma((3, 2)),
            dma((3, 2)),
            dma((len(spans),)),
            dma((len(spans),)),
            dma((lines - 1, len(spans))),
            dma((lines - 1, len(spans))),
        ],
        compiler_params=pltpu.CompilerParams(
            collective_id=0, has_side_effects=True, vmem_limit_bytes=56 << 20
        ),
        cost_estimate=pl.CostEstimate(
            flops=6 * row_count * units * model_width,
            bytes_accessed=32 << 20,
            transcendentals=0,
        ),
        name="layer",
    )(tokens, out_grad, picks, gates, counts, weight_in, weight_out)


def local(tokens, out_grad, gates, picks, counts, w_in, w_out):
    t_dev, model_width = tokens.shape
    slot_count = picks.shape[2]
    parts = lax.axis_size("dp")
    count = lax.axis_size("expert")
    row_count = count * slot_count
    slices, all_pre, all_hidden, summed_rows, summed_gates = layer(
        tokens, out_grad, picks[0], gates[0], counts, w_in[0], w_out[0], count, parts
    )

    def weight_grad(columns, units):
        return lax.dot_general(
            columns.reshape(parts * row_count, model_width // parts),
            units.reshape(parts * row_count, units.shape[-1]),
            (((0,), (0,)), ((), ())),
            preferred_element_type=jnp.float32,
        ).astype(jnp.bfloat16)[None]

    chosen = (picks[0, 0][:, None] == jnp.arange(t_dev)[None, :]).astype(jnp.bfloat16)
    tokens_grad = lax.dot_general(
        chosen, summed_rows, (((0,), (0,)), ((), ())), preferred_element_type=jnp.float32
    ).astype(jnp.bfloat16)
    live = jnp.arange(slot_count)[None, :] < counts[0][:, None]
    gates_grad = jnp.where(live, summed_gates[:, 0][None], 0.0)[None]
    return (
        tokens_grad,
        gates_grad,
        weight_grad(slices[0], all_pre),
        weight_grad(slices[1], all_hidden),
    )


def local_many(tokens, out_grad, gates, picks, counts, w_in, w_out):
    t_dev, model_width = tokens.shape
    expert_count = picks.shape[1]
    slot_count = picks.shape[2]
    part_units = w_in.shape[2]
    part_count = FF // part_units
    expert_devices = lax.axis_size("expert")
    row_index = picks[0].reshape(-1)
    live = jnp.arange(slot_count)[None, :] < counts[0][:, None]
    scale = jnp.where(live, gates[0], jnp.zeros_like(gates[0]))

    def exchange(values):
        return lax.all_to_all(values, "expert", split_axis=0, concat_axis=0, tiled=True)

    def spread(values):
        wide = jnp.broadcast_to(values[:, None], (expert_count, part_count) + values.shape[1:])
        return exchange(wide.reshape((expert_devices,) + values.shape[1:]))

    row_count = expert_devices * slot_count
    picked_shape = (expert_count, slot_count, model_width)
    rows_x = spread(tokens[row_index].reshape(picked_shape)).reshape(row_count, model_width)
    rows_dy = spread(out_grad[row_index].reshape(picked_shape)).reshape(row_count, model_width)
    row_scale = spread(scale).reshape(row_count, 1).astype(jnp.float32)
    weight_in, weight_out = w_in[0], w_out[0]
    pre = jnp.dot(rows_x, weight_in, preferred_element_type=jnp.float32)
    back = jnp.dot(rows_dy, weight_out, preferred_element_type=jnp.float32)
    hidden, gelu_back = jax.vjp(jax.nn.gelu, pre)
    gate_part = jnp.sum(hidden * back, axis=-1)
    pre_grad = gelu_back(row_scale * back)[0].astype(jnp.bfloat16)
    scaled_hidden = (row_scale * hidden).astype(jnp.bfloat16)
    row_part = lax.dot_general(
        pre_grad, weight_in, (((1,), (1,)), ((), ())), preferred_element_type=jnp.float32
    )

    def weight_grad(columns, units):
        columns = lax.all_to_all(columns, "dp", split_axis=1, concat_axis=0, tiled=True)
        units = lax.all_gather(units, "dp", axis=0, tiled=True)
        return lax.dot_general(
            columns, units, (((0,), (0,)), ((), ())), preferred_element_type=jnp.float32
        ).astype(jnp.bfloat16)[None]

    back_shape = (expert_devices, slot_count, model_width)
    back_rows = exchange(row_part.reshape(back_shape).astype(jnp.bfloat16)).astype(jnp.float32)
    back_gates = exchange(gate_part.reshape(back_shape[:2]))
    summed_rows = jnp.sum(back_rows.reshape((expert_count, part_count) + back_shape[1:]), axis=1)
    summed_gates = jnp.sum(back_gates.reshape(expert_count, part_count, slot_count), axis=1)
    empty_rows = jnp.zeros((t_dev, model_width), jnp.float32)
    tokens_grad = (
        empty_rows.at[row_index].add(summed_rows.reshape(-1, model_width)).astype(jnp.bfloat16)
    )
    gates_grad = jnp.where(live, summed_gates, jnp.zeros_like(summed_gates))[None]
    return (
        tokens_grad,
        gates_grad,
        weight_grad(rows_x, pre_grad),
        weight_grad(rows_dy, scaled_hidden),
    )


def solution(mesh):
    placed = (
        P(("expert", "dp"), None),
        P(("expert", "dp"), None),
        P(("expert", "dp"), None, None),
        P(("expert", "dp"), None, None),
        P(("expert", "dp"), None),
        P("expert", None, None),
        P("expert", None, None),
    )

    def run(*arrays):
        one = arrays[3].shape[1] == 1 and mesh.shape["dp"] == 4
        return jax.shard_map(
            local if one else local_many,
            mesh=mesh,
            in_specs=placed,
            out_specs=(
                P(("expert", "dp"), None),
                P(("expert", "dp"), None, None),
                P("expert", "dp", None),
                P("expert", "dp", None),
            ),
            check_vma=False,
        )(*arrays)

    return run
```

```python
import functools

import jax
import jax.numpy as jnp
from jax import lax
from jax.experimental import pallas as pl
from jax.experimental.pallas import tpu as pltpu
from jax.sharding import PartitionSpec as P

FF = 8192
LANES = 128
ROOT = 0.7978845608028654
CUBE = 0.044715
MESH = pl.DeviceIdType.MESH


def meet(peers):
    barrier = pltpu.get_barrier_semaphore()
    for peer in peers:
        pl.semaphore_signal(barrier, inc=1, device_id=peer, device_id_type=MESH)
    pl.semaphore_wait(barrier, len(peers))


def send(src, dst, send_sem, recv_sem, peer):
    copy = pltpu.make_async_remote_copy(
        src_ref=src,
        dst_ref=dst,
        send_sem=send_sem,
        recv_sem=recv_sem,
        device_id=peer,
        device_id_type=MESH,
    )
    copy.start()
    return copy


def layer_kernel(
    spans,
    tokens,
    out_grad,
    picks,
    gates,
    counts,
    weight_in,
    weight_out,
    slices,
    all_pre,
    all_hidden,
    rows_out,
    gates_out,
    tables,
    w1,
    w2,
    rows,
    scales,
    pre,
    back,
    gate,
    pre_grad,
    hidden,
    terms,
    beside_terms,
    pair_sum,
    line_terms,
    table_sem,
    w_sem,
    s_send,
    s_recv,
    g_send,
    g_recv,
    gx_send,
    gx_recv,
    dp_send,
    dp_recv,
    keep_sem,
    own_sem,
    a_send,
    a_recv,
    x_send,
    x_recv,
    z_send,
    z_recv,
):
    parts = all_pre.shape[0]
    lines, _, slots, model_width = rows.shape[1:]
    count = 2 * lines
    pair_rows = 2 * slots
    width = model_width // parts
    e = lax.axis_index("expert")
    d = lax.axis_index("dp")
    z = e // 2
    x = lax.rem(e, 2)
    after = lax.rem(e + 2, count)
    beside = e + 1 - 2 * x
    twin = d + 1 - 2 * lax.rem(d, 2)
    across = lax.rem(d + 2, parts)
    loads = [
        pltpu.make_async_copy(src, tables.at[i], table_sem.at[i])
        for i, src in enumerate((tokens, out_grad))
    ] + [
        pltpu.make_async_copy(src, dst, w_sem.at[i])
        for i, (src, dst) in enumerate(((weight_in, w1), (weight_out, w2)))
    ]
    for copy in loads:
        copy.start()
    group = [lax.rem(e + 2 * t, count) for t in range(1, lines)]
    group += [lax.rem(beside + 2 * t, count) for t in range(lines)]
    meet([(peer, d) for peer in group] + [(e, lax.rem(d + k, parts)) for k in range(1, parts)])
    sent = []

    def line(s):
        return lax.rem(z + lines - s, lines)

    def block(zz, xx, c):
        return rows.at[:, zz, xx, :, pl.ds(c * width, width)]

    def to_z(s, c):
        ref = block(line(s), x, c)
        sent.append(send(ref, ref, g_send.at[s, c], g_recv.at[s, c], (after, d)))

    def to_beside(s, c):
        ref = block(line(s), x, c)
        sent.append(send(ref, ref, gx_send.at[s, c], gx_recv.at[s, c], (beside, d)))

    def to_dp(s, xx, c):
        ref = block(line(s), xx, c)

        @pl.when(d == c)
        def _():
            pltpu.make_async_copy(ref, slices.at[:, d, line(s), xx], keep_sem).start()

        @pl.when(d != c)
        def _():
            send(ref, slices.at[:, d, line(s), xx], dp_send, dp_recv.at[d], (e, c))

    def arrived(ref, sem):
        pltpu.make_async_copy(ref, ref, sem).wait()

    chosen = lax.broadcasted_iota(jnp.int32, (tables.shape[1], slots), 0) == picks[...]
    chosen = chosen.astype(jnp.float32).astype(jnp.bfloat16)
    for copy in loads[:2]:
        copy.wait()
    for c in range(parts):
        cols = slice(c * width, (c + 1) * width)
        for i in range(2):
            rows[i, z, x, :, cols] = lax.dot_general(
                chosen,
                tables[i, :, cols],
                (((0,), (0,)), ((), ())),
                preferred_element_type=jnp.float32,
            ).astype(jnp.bfloat16)
        to_beside(0, c)
        to_z(0, c)
        to_dp(0, x, c)
    slot = lax.broadcasted_iota(jnp.int32, (slots, slots), 1)
    live = slot == lax.broadcasted_iota(jnp.int32, (slots, slots), 0)
    live = jnp.logical_and(live, slot < counts[...])
    scale = jnp.where(live, jnp.broadcast_to(gates[...].astype(jnp.float32), (slots, slots)), 0.0)
    scale = jnp.sum(scale, axis=1, keepdims=True)
    scales[e] = jnp.broadcast_to(scale, (slots, LANES))
    for i, peer in enumerate(group):
        sent.append(send(scales.at[e], scales.at[e], s_send.at[i], s_recv.at[e], (peer, d)))

    pairs = ((pre_grad, all_pre), (hidden, all_hidden))

    def forward(s):
        for c in range(parts):
            arrived(block(line(s), x, c), g_recv.at[s - 1, c])
            if s < lines - 1:
                to_z(s, c)
            to_beside(s, c)
            to_dp(s, x, c)

    def multiply(s):
        for c in range(parts):
            arrived(block(line(s), 1 - x, c), gx_recv.at[s, c])
            to_dp(s, 1 - x, c)
            if s == 0 and c == 0:
                for copy in loads[2:]:
                    copy.wait()
            cols = slice(c * width, (c + 1) * width)
            for i, (weight, total) in enumerate(((w1, pre), (w2, back))):
                part = rows[i, line(s), :, :, cols].astype(jnp.float32).reshape(pair_rows, width)
                part = jnp.dot(
                    part.astype(jnp.bfloat16), weight[cols, :], preferred_element_type=jnp.float32
                )
                if c == 0:
                    total[...] = part
                else:
                    total[...] += part

    def activate(s):
        zz = line(s)
        for owner in (2 * zz + x, 2 * zz + 1 - x)[s == 0 :]:
            arrived(scales.at[owner], s_recv.at[owner])
        row_scale = scales[pl.ds(2 * zz, 2)].reshape(pair_rows, LANES)
        step = 16
        for start in range(0, pair_rows, step):
            here = slice(start, start + step)
            v, g, scale = pre[here, :], back[here, :], row_scale[here, :1]
            square = v * v
            bend = jnp.tanh(ROOT * v * (1.0 + CUBE * square))
            half = 0.5 * (1.0 + bend)
            value = v * half
            slope = half + 0.5 * v * (1.0 - bend * bend) * ROOT * (1.0 + 3.0 * CUBE * square)
            pre_grad[zz, here, :] = (scale * g * slope).astype(jnp.bfloat16)
            hidden[zz, here, :] = (scale * value).astype(jnp.bfloat16)
            gate[here, :] = jnp.broadcast_to(
                jnp.sum(value * g, axis=1, keepdims=True), (step, LANES)
            )
        for i, (src, dst) in enumerate(pairs):
            for hop, peer in ((0, across), (1, twin)):
                sems = a_send.at[hop, s, i], a_recv.at[hop, s, i]
                sent.append(send(src.at[zz], dst.at[d, zz], *sems, (e, peer)))

    def pass_on(s):
        for i, (_, dst) in enumerate(pairs):
            ref = dst.at[across, line(s)]
            arrived(ref, a_recv.at[0, s, i])
            sent.append(send(ref, ref, a_send.at[2, s, i], a_recv.at[2, s, i], (e, twin)))

    def give_back(s):
        zz = line(s)
        value = gate[...].reshape(2, slots, LANES).astype(jnp.bfloat16)
        terms[zz, :, :, model_width:] = value
        for c in range(parts):
            cols = slice(c * width, (c + 1) * width)
            value = lax.dot_general(
                pre_grad[zz],
                w1[cols, :],
                (((1,), (1,)), ((), ())),
                preferred_element_type=jnp.float32,
            )
            terms[zz, :, :, cols] = value.reshape(2, slots, width).astype(jnp.bfloat16)
            for k, (start, size) in enumerate(spans):
                if (c + 1) * width == min(start + size, model_width):
                    here = pl.ds(start, size)
                    sent.append(
                        send(
                            terms.at[zz, 1 - x, :, here],
                            beside_terms.at[zz, :, here],
                            x_send.at[s, k],
                            x_recv.at[s, k],
                            (beside, d),
                        )
                    )

    def to_line(s):
        zz = line(s)
        for k, (start, size) in enumerate(spans):
            cols = slice(start, start + size)
            here = pl.ds(start, size)
            arrived(beside_terms.at[zz, :, here], x_recv.at[s, k])
            if s > 0:
                total = terms[zz, x, :, cols].astype(jnp.float32)
                total += beside_terms[zz, :, cols].astype(jnp.float32)
                pair_sum[s - 1, :, cols] = total.astype(jnp.bfloat16)
                sent.append(
                    send(
                        pair_sum.at[s - 1, :, here],
                        line_terms.at[s - 1, :, here],
                        z_send.at[s - 1, k],
                        z_recv.at[s - 1, k],
                        (2 * zz + x, d),
                    )
                )

    for s in range(lines):
        if s < lines - 1:
            forward(s + 1)
        multiply(s)
        activate(s)
        give_back(s)
        if s > 0:
            to_line(s - 1)
            pass_on(s - 1)
    for i, (src, dst) in enumerate(pairs):
        pltpu.make_async_copy(src, dst.at[d], own_sem.at[i]).start()
    to_line(lines - 1)
    pass_on(lines - 1)
    for k, (start, size) in enumerate(spans):
        cols = slice(start, start + size)
        total = terms[z, x, :, cols].astype(jnp.float32)
        total += beside_terms[z, :, cols].astype(jnp.float32)
        for s in range(1, lines):
            arrived(line_terms.at[s - 1, :, pl.ds(start, size)], z_recv.at[s - 1, k])
            total += line_terms[s - 1, :, cols].astype(jnp.float32)
        inside = min(size, model_width - start)
        rows_out[:, start : start + inside] = total[:, :inside].astype(jnp.bfloat16)
        if inside < size:
            gates_out[...] = total[:, inside:]
    for i, (src, dst) in enumerate(pairs):
        pltpu.make_async_copy(src, dst.at[d], own_sem.at[i]).wait()
        for hop, owner in ((1, twin), (2, lax.rem(twin + 2, parts))):
            for s in range(lines):
                arrived(dst.at[owner, line(s)], a_recv.at[hop, s, i])
    for copy in sent:
        copy.wait_send()
    arrived(slices.at[:, pl.ds(0, parts - 1)], dp_send)
    arrived(slices.at[:, d], keep_sem)
    for k in range(1, parts):
        owner = lax.rem(d + k, parts)
        arrived(slices.at[:, owner], dp_recv.at[owner])


def layer(tokens, out_grad, picks, gates, counts, weight_in, weight_out, count, parts):
    t_dev, model_width = tokens.shape
    slots = picks.shape[-1]
    units = weight_in.shape[1]
    row_count = count * slots
    lines = count // 2
    width = model_width // parts
    wide = model_width + LANES
    half = model_width // 2
    spans = [(0, half), (half, wide - half)]
    pair_rows = 2 * slots
    dma = pltpu.SemaphoreType.DMA
    vmem = pl.BlockSpec(memory_space=pltpu.VMEM)
    anywhere = pl.BlockSpec(memory_space=pl.ANY)
    bf16, f32 = jnp.bfloat16, jnp.float32
    return pl.pallas_call(
        functools.partial(layer_kernel, spans),
        out_shape=(
            jax.ShapeDtypeStruct((2, parts, lines, 2, slots, width), bf16),
            jax.ShapeDtypeStruct((parts, lines, pair_rows, units), bf16),
            jax.ShapeDtypeStruct((parts, lines, pair_rows, units), bf16),
            jax.ShapeDtypeStruct((slots, model_width), bf16),
            jax.ShapeDtypeStruct((slots, LANES), f32),
        ),
        in_specs=[anywhere, anywhere, vmem, vmem, vmem, anywhere, anywhere],
        out_specs=[anywhere, anywhere, anywhere, vmem, vmem],
        scratch_shapes=[
            pltpu.VMEM((2, t_dev, model_width), bf16),
            pltpu.VMEM((model_width, units), bf16),
            pltpu.VMEM((model_width, units), bf16),
            pltpu.VMEM((2, lines, 2, slots, model_width), bf16),
            pltpu.VMEM((count, slots, LANES), f32),
            pltpu.VMEM((pair_rows, units), f32),
            pltpu.VMEM((pair_rows, units), f32),
            pltpu.VMEM((pair_rows, LANES), f32),
            pltpu.VMEM((lines, pair_rows, units), bf16),
            pltpu.VMEM((lines, pair_rows, units), bf16),
            pltpu.VMEM((lines, 2, slots, wide), bf16),
            pltpu.VMEM((lines, slots, wide), bf16),
            pltpu.VMEM((lines - 1, slots, wide), bf16),
            pltpu.VMEM((lines - 1, slots, wide), bf16),
            dma((2,)),
            dma((2,)),
            dma((count - 1,)),
            dma((count,)),
            dma((lines - 1, parts)),
            dma((lines - 1, parts)),
            dma((lines, parts)),
            dma((lines, parts)),
            dma,
            dma((parts,)),
            dma,
            dma((2,)),
            dma((3, lines, 2)),
            dma((3, lines, 2)),
            dma((lines, len(spans))),
            dma((lines, len(spans))),
            dma((lines - 1, len(spans))),
            dma((lines - 1, len(spans))),
        ],
        compiler_params=pltpu.CompilerParams(
            collective_id=0, has_side_effects=True, vmem_limit_bytes=56 << 20
        ),
        cost_estimate=pl.CostEstimate(
            flops=6 * row_count * units * model_width,
            bytes_accessed=32 << 20,
            transcendentals=0,
        ),
        name="layer",
    )(tokens, out_grad, picks, gates, counts, weight_in, weight_out)


def local(tokens, out_grad, gates, picks, counts, w_in, w_out):
    t_dev, model_width = tokens.shape
    slot_count = picks.shape[2]
    parts = lax.axis_size("dp")
    count = lax.axis_size("expert")
    row_count = count * slot_count
    slices, all_pre, all_hidden, summed_rows, summed_gates = layer(
        tokens, out_grad, picks[0], gates[0], counts, w_in[0], w_out[0], count, parts
    )

    def weight_grad(columns, units):
        return lax.dot_general(
            columns.reshape(parts * row_count, model_width // parts),
            units.reshape(parts * row_count, units.shape[-1]),
            (((0,), (0,)), ((), ())),
            preferred_element_type=jnp.float32,
        ).astype(jnp.bfloat16)[None]

    chosen = (picks[0, 0][:, None] == jnp.arange(t_dev)[None, :]).astype(jnp.bfloat16)
    tokens_grad = lax.dot_general(
        chosen, summed_rows, (((0,), (0,)), ((), ())), preferred_element_type=jnp.float32
    ).astype(jnp.bfloat16)
    live = jnp.arange(slot_count)[None, :] < counts[0][:, None]
    gates_grad = jnp.where(live, summed_gates[:, 0][None], 0.0)[None]
    return (
        tokens_grad,
        gates_grad,
        weight_grad(slices[0], all_pre),
        weight_grad(slices[1], all_hidden),
    )


def local_many(tokens, out_grad, gates, picks, counts, w_in, w_out):
    t_dev, model_width = tokens.shape
    expert_count = picks.shape[1]
    slot_count = picks.shape[2]
    part_units = w_in.shape[2]
    part_count = FF // part_units
    expert_devices = lax.axis_size("expert")
    row_index = picks[0].reshape(-1)
    live = jnp.arange(slot_count)[None, :] < counts[0][:, None]
    scale = jnp.where(live, gates[0], jnp.zeros_like(gates[0]))

    def exchange(values):
        return lax.all_to_all(values, "expert", split_axis=0, concat_axis=0, tiled=True)

    def spread(values):
        wide = jnp.broadcast_to(values[:, None], (expert_count, part_count) + values.shape[1:])
        return exchange(wide.reshape((expert_devices,) + values.shape[1:]))

    row_count = expert_devices * slot_count
    picked_shape = (expert_count, slot_count, model_width)
    rows_x = spread(tokens[row_index].reshape(picked_shape)).reshape(row_count, model_width)
    rows_dy = spread(out_grad[row_index].reshape(picked_shape)).reshape(row_count, model_width)
    row_scale = spread(scale).reshape(row_count, 1).astype(jnp.float32)
    weight_in, weight_out = w_in[0], w_out[0]
    pre = jnp.dot(rows_x, weight_in, preferred_element_type=jnp.float32)
    back = jnp.dot(rows_dy, weight_out, preferred_element_type=jnp.float32)
    hidden, gelu_back = jax.vjp(jax.nn.gelu, pre)
    gate_part = jnp.sum(hidden * back, axis=-1)
    pre_grad = gelu_back(row_scale * back)[0].astype(jnp.bfloat16)
    scaled_hidden = (row_scale * hidden).astype(jnp.bfloat16)
    row_part = lax.dot_general(
        pre_grad, weight_in, (((1,), (1,)), ((), ())), preferred_element_type=jnp.float32
    )

    def weight_grad(columns, units):
        columns = lax.all_to_all(columns, "dp", split_axis=1, concat_axis=0, tiled=True)
        units = lax.all_gather(units, "dp", axis=0, tiled=True)
        return lax.dot_general(
            columns, units, (((0,), (0,)), ((), ())), preferred_element_type=jnp.float32
        ).astype(jnp.bfloat16)[None]

    back_shape = (expert_devices, slot_count, model_width)
    back_rows = exchange(row_part.reshape(back_shape).astype(jnp.bfloat16)).astype(jnp.float32)
    back_gates = exchange(gate_part.reshape(back_shape[:2]))
    summed_rows = jnp.sum(back_rows.reshape((expert_count, part_count) + back_shape[1:]), axis=1)
    summed_gates = jnp.sum(back_gates.reshape(expert_count, part_count, slot_count), axis=1)
    empty_rows = jnp.zeros((t_dev, model_width), jnp.float32)
    tokens_grad = (
        empty_rows.at[row_index].add(summed_rows.reshape(-1, model_width)).astype(jnp.bfloat16)
    )
    gates_grad = jnp.where(live, summed_gates, jnp.zeros_like(summed_gates))[None]
    return (
        tokens_grad,
        gates_grad,
        weight_grad(rows_x, pre_grad),
        weight_grad(rows_dy, scaled_hidden),
    )


def solution(mesh):
    placed = (
        P(("expert", "dp"), None),
        P(("expert", "dp"), None),
        P(("expert", "dp"), None, None),
        P(("expert", "dp"), None, None),
        P(("expert", "dp"), None),
        P("expert", None, None),
        P("expert", None, None),
    )

    def run(*arrays):
        one = arrays[3].shape[1] == 1 and mesh.shape["dp"] == 4
        return jax.shard_map(
            local if one else local_many,
            mesh=mesh,
            in_specs=placed,
            out_specs=(
                P(("expert", "dp"), None),
                P(("expert", "dp"), None, None),
                P("expert", "dp", None),
                P("expert", "dp", None),
            ),
            check_vma=False,
        )(*arrays)

    return run
```

```python
import functools

import jax
import jax.numpy as jnp
from jax import lax
from jax.experimental import pallas as pl
from jax.experimental.pallas import tpu as pltpu
from jax.sharding import PartitionSpec as P

FF = 8192
LANES = 128
ROOT = 0.7978845608028654
CUBE = 0.044715
MESH = pl.DeviceIdType.MESH


def meet(peers):
    barrier = pltpu.get_barrier_semaphore()
    for peer in peers:
        pl.semaphore_signal(barrier, inc=1, device_id=peer, device_id_type=MESH)
    pl.semaphore_wait(barrier, len(peers))


def send(src, dst, send_sem, recv_sem, peer):
    copy = pltpu.make_async_remote_copy(
        src_ref=src,
        dst_ref=dst,
        send_sem=send_sem,
        recv_sem=recv_sem,
        device_id=peer,
        device_id_type=MESH,
    )
    copy.start()
    return copy


def layer_kernel(
    spans,
    tokens,
    out_grad,
    picks,
    gates,
    counts,
    weight_in,
    weight_out,
    x_slices,
    dy_slices,
    all_pre,
    all_hidden,
    rows_out,
    gates_out,
    tables,
    w1,
    w2,
    rows,
    scales,
    pre,
    back,
    gate,
    pre_grad,
    hidden,
    terms,
    beside_terms,
    pair_sum,
    line_terms,
    table_sem,
    w_sem,
    s_send,
    s_recv,
    g_send,
    g_recv,
    gx_send,
    gx_recv,
    dp_send,
    dp_recv,
    keep_sem,
    own_sem,
    a_send,
    a_recv,
    x_send,
    x_recv,
    z_send,
    z_recv,
):
    parts = all_pre.shape[0]
    lines, _, slots, model_width = rows.shape[1:]
    count = 2 * lines
    pair_rows = 2 * slots
    width = model_width // parts
    e = lax.axis_index("expert")
    d = lax.axis_index("dp")
    z = e // 2
    x = lax.rem(e, 2)
    after = lax.rem(e + 2, count)
    beside = e + 1 - 2 * x
    twin = d + 1 - 2 * lax.rem(d, 2)
    across = lax.rem(d + 2, parts)
    loads = [
        pltpu.make_async_copy(src, tables.at[i], table_sem.at[i])
        for i, src in enumerate((tokens, out_grad))
    ] + [
        pltpu.make_async_copy(src, dst, w_sem.at[i])
        for i, (src, dst) in enumerate(((weight_in, w1), (weight_out, w2)))
    ]
    for copy in loads:
        copy.start()
    group = [lax.rem(e + 2 * t, count) for t in range(1, lines)]
    group += [lax.rem(beside + 2 * t, count) for t in range(lines)]
    meet([(peer, d) for peer in group] + [(e, lax.rem(d + k, parts)) for k in range(1, parts)])
    sent = []

    def line(s):
        return lax.rem(z + lines - s, lines)

    def block(zz, xx, c):
        return rows.at[:, zz, xx, :, pl.ds(c * width, width)]

    def to_z(s, c):
        ref = block(line(s), x, c)
        sent.append(send(ref, ref, g_send.at[s, c], g_recv.at[s, c], (after, d)))

    def to_beside(s, c):
        ref = block(line(s), x, c)
        sent.append(send(ref, ref, gx_send.at[s, c], gx_recv.at[s, c], (beside, d)))

    def to_dp(s, pick):
        for c in range(parts):
            for i, slices in enumerate((x_slices, dy_slices)):
                ref = rows.at[i, line(s), pick, :, pl.ds(c * width, width)]

                @pl.when(d == c)
                def _():
                    mine = slices.at[d, line(s), pick]
                    pltpu.make_async_copy(ref, mine, keep_sem.at[i]).start()

                @pl.when(d != c)
                def _():
                    there = slices.at[d, line(s), pick]
                    send(ref, there, dp_send.at[i], dp_recv.at[i, d], (e, c))

    def arrived(ref, sem):
        pltpu.make_async_copy(ref, ref, sem).wait()

    chosen = lax.broadcasted_iota(jnp.int32, (tables.shape[1], slots), 0) == picks[...]
    chosen = chosen.astype(jnp.float32).astype(jnp.bfloat16)
    for copy in loads[:2]:
        copy.wait()
    for c in range(parts):
        cols = slice(c * width, (c + 1) * width)
        for i in range(2):
            rows[i, z, x, :, cols] = lax.dot_general(
                chosen,
                tables[i, :, cols],
                (((0,), (0,)), ((), ())),
                preferred_element_type=jnp.float32,
            ).astype(jnp.bfloat16)
        to_beside(0, c)
        to_z(0, c)
    to_dp(0, x)
    slot = lax.broadcasted_iota(jnp.int32, (slots, slots), 1)
    live = slot == lax.broadcasted_iota(jnp.int32, (slots, slots), 0)
    live = jnp.logical_and(live, slot < counts[...])
    scale = jnp.where(live, jnp.broadcast_to(gates[...].astype(jnp.float32), (slots, slots)), 0.0)
    scale = jnp.sum(scale, axis=1, keepdims=True)
    scales[e] = jnp.broadcast_to(scale, (slots, LANES))
    for i, peer in enumerate(group):
        sent.append(send(scales.at[e], scales.at[e], s_send.at[i], s_recv.at[e], (peer, d)))

    pairs = ((pre_grad, all_pre), (hidden, all_hidden))

    def forward(s):
        for c in range(parts):
            arrived(block(line(s), x, c), g_recv.at[s - 1, c])
            if s < lines - 1:
                to_z(s, c)
            to_beside(s, c)

    def collect(s, pick):
        for c in range(parts):
            arrived(block(line(s), 1 - x, c), gx_recv.at[s, c])
        to_dp(s, pick)

    def multiply(group):
        if group[0] == 0:
            for copy in loads[2:]:
                copy.wait()
        for c in range(parts):
            cols = slice(c * width, (c + 1) * width)
            for i, (weight, total) in enumerate(((w1, pre), (w2, back))):
                part = jnp.concatenate(
                    [
                        rows[i, line(s), :, :, cols].astype(jnp.float32).reshape(pair_rows, width)
                        for s in group
                    ]
                )
                part = jnp.dot(
                    part.astype(jnp.bfloat16), weight[cols, :], preferred_element_type=jnp.float32
                )
                if c == 0:
                    total[...] = part
                else:
                    total[...] += part

    def activate(group):
        for j, s in enumerate(group):
            zz = line(s)
            for owner in (2 * zz + x, 2 * zz + 1 - x)[s == 0 :]:
                arrived(scales.at[owner], s_recv.at[owner])
            row_scale = scales[pl.ds(2 * zz, 2)].reshape(pair_rows, LANES)
            step = 16
            for start in range(0, pair_rows, step):
                here = slice(start, start + step)
                there = slice(j * pair_rows + start, j * pair_rows + start + step)
                v, g, scale = pre[there, :], back[there, :], row_scale[here, :1]
                square = v * v
                bend = jnp.tanh(ROOT * v * (1.0 + CUBE * square))
                half = 0.5 * (1.0 + bend)
                value = v * half
                slope = half + 0.5 * v * (1.0 - bend * bend) * ROOT * (1.0 + 3.0 * CUBE * square)
                pre_grad[zz, here, :] = (scale * g * slope).astype(jnp.bfloat16)
                hidden[zz, here, :] = (scale * value).astype(jnp.bfloat16)
                gate[there, :] = jnp.broadcast_to(
                    jnp.sum(value * g, axis=1, keepdims=True), (step, LANES)
                )
            for i, (src, dst) in enumerate(pairs):
                for hop, peer in ((0, across), (1, twin)):
                    sems = a_send.at[hop, s, i], a_recv.at[hop, s, i]
                    sent.append(send(src.at[zz], dst.at[d, zz], *sems, (e, peer)))

    def pass_on(s):
        for i, (_, dst) in enumerate(pairs):
            ref = dst.at[across, line(s)]
            arrived(ref, a_recv.at[0, s, i])
            sent.append(send(ref, ref, a_send.at[2, s, i], a_recv.at[2, s, i], (e, twin)))

    def give_back(group):
        units = jnp.concatenate([pre_grad[line(s)] for s in group])

        def keep(cols, value):
            size = value.shape[-1]
            value = value.reshape(len(group), 2, slots, size).astype(jnp.bfloat16)
            for j, s in enumerate(group):
                terms[line(s), :, :, cols] = value[j]

        keep(slice(model_width, model_width + LANES), gate[...])
        for k, (start, size) in enumerate(spans):
            cols = slice(start, start + width)
            value = lax.dot_general(
                units, w1[cols, :], (((1,), (1,)), ((), ())), preferred_element_type=jnp.float32
            )
            keep(cols, value)
            here = pl.ds(start, size)
            for s in group:
                sent.append(
                    send(
                        terms.at[line(s), 1 - x, :, here],
                        beside_terms.at[line(s), :, here],
                        x_send.at[s, k],
                        x_recv.at[s, k],
                        (beside, d),
                    )
                )

    def to_line(s, k):
        zz = line(s)
        start, size = spans[k]
        cols = slice(start, start + size)
        here = pl.ds(start, size)
        arrived(beside_terms.at[zz, :, here], x_recv.at[s, k])
        if s > 0:
            total = terms[zz, x, :, cols].astype(jnp.float32)
            total += beside_terms[zz, :, cols].astype(jnp.float32)
            pair_sum[s - 1, :, cols] = total.astype(jnp.bfloat16)
            sent.append(
                send(
                    pair_sum.at[s - 1, :, here],
                    line_terms.at[s - 1, :, here],
                    z_send.at[s - 1, k],
                    z_recv.at[s - 1, k],
                    (2 * zz + x, d),
                )
            )

    early, late = range(lines // 2), range(lines // 2, lines)
    for s in early:
        if s > 0:
            forward(s)
            to_dp(s, x)
    for s in early:
        if s == early[-1]:
            forward(s + 1)
        collect(s, 1 - x)
    multiply(early)
    activate(early)
    for s in late:
        if s > late[0]:
            forward(s)
    give_back(early)
    for s in late:
        collect(s, slice(None))
    multiply(late)
    activate(late)
    for s in early:
        for k in range(len(spans)):
            to_line(s, k)
    give_back(late)
    for i, (src, dst) in enumerate(pairs):
        pltpu.make_async_copy(src, dst.at[d], own_sem.at[i]).start()
    for s in early:
        pass_on(s)
    for k in range(len(spans)):
        for s in late:
            to_line(s, k)
    for s in late:
        pass_on(s)
    for k, (start, size) in enumerate(spans):
        cols = slice(start, start + size)
        total = terms[z, x, :, cols].astype(jnp.float32)
        total += beside_terms[z, :, cols].astype(jnp.float32)
        for s in range(1, lines):
            arrived(line_terms.at[s - 1, :, pl.ds(start, size)], z_recv.at[s - 1, k])
            total += line_terms[s - 1, :, cols].astype(jnp.float32)
        inside = min(size, model_width - start)
        rows_out[:, start : start + inside] = total[:, :inside].astype(jnp.bfloat16)
        if inside < size:
            own = jnp.logical_and(
                slot == lax.broadcasted_iota(jnp.int32, (slots, slots), 0), slot < counts[...]
            )
            total = jnp.where(own, total[:, inside : inside + 1], 0.0)
            gates_out[...] = jnp.sum(total, axis=0, keepdims=True)
    for i, (src, dst) in enumerate(pairs):
        pltpu.make_async_copy(src, dst.at[d], own_sem.at[i]).wait()
        for hop, owner in ((1, twin), (2, lax.rem(twin + 2, parts))):
            for s in range(lines):
                arrived(dst.at[owner, line(s)], a_recv.at[hop, s, i])
    for copy in sent:
        copy.wait_send()
    for i, slices in enumerate((x_slices, dy_slices)):
        arrived(slices.at[pl.ds(0, parts - 1)], dp_send.at[i])
        arrived(slices.at[d], keep_sem.at[i])
        for k in range(1, parts):
            owner = lax.rem(d + k, parts)
            arrived(slices.at[owner], dp_recv.at[i, owner])


def layer(tokens, out_grad, picks, gates, counts, weight_in, weight_out, count, parts):
    t_dev, model_width = tokens.shape
    slots = picks.shape[-1]
    units = weight_in.shape[1]
    row_count = count * slots
    lines = count // 2
    width = model_width // parts
    wide = model_width + LANES
    spans = [(k * width, width) for k in range(parts - 1)]
    spans.append((model_width - width, width + LANES))
    pair_rows = 2 * slots
    dma = pltpu.SemaphoreType.DMA
    vmem = pl.BlockSpec(memory_space=pltpu.VMEM)
    anywhere = pl.BlockSpec(memory_space=pl.ANY)
    bf16, f32 = jnp.bfloat16, jnp.float32
    return pl.pallas_call(
        functools.partial(layer_kernel, spans),
        out_shape=(
            jax.ShapeDtypeStruct((parts, lines, 2, slots, width), bf16),
            jax.ShapeDtypeStruct((parts, lines, 2, slots, width), bf16),
            jax.ShapeDtypeStruct((parts, lines, pair_rows, units), bf16),
            jax.ShapeDtypeStruct((parts, lines, pair_rows, units), bf16),
            jax.ShapeDtypeStruct((slots, model_width), bf16),
            jax.ShapeDtypeStruct((1, slots), f32),
        ),
        in_specs=[anywhere, anywhere, vmem, vmem, vmem, anywhere, anywhere],
        out_specs=[anywhere, anywhere, anywhere, anywhere, vmem, vmem],
        scratch_shapes=[
            pltpu.VMEM((2, t_dev, model_width), bf16),
            pltpu.VMEM((model_width, units), bf16),
            pltpu.VMEM((model_width, units), bf16),
            pltpu.VMEM((2, lines, 2, slots, model_width), bf16),
            pltpu.VMEM((count, slots, LANES), f32),
            pltpu.VMEM((row_count // 2, units), f32),
            pltpu.VMEM((row_count // 2, units), f32),
            pltpu.VMEM((row_count // 2, LANES), f32),
            pltpu.VMEM((lines, pair_rows, units), bf16),
            pltpu.VMEM((lines, pair_rows, units), bf16),
            pltpu.VMEM((lines, 2, slots, wide), bf16),
            pltpu.VMEM((lines, slots, wide), bf16),
            pltpu.VMEM((lines - 1, slots, wide), bf16),
            pltpu.VMEM((lines - 1, slots, wide), bf16),
            dma((2,)),
            dma((2,)),
            dma((count - 1,)),
            dma((count,)),
            dma((lines - 1, parts)),
            dma((lines - 1, parts)),
            dma((lines, parts)),
            dma((lines, parts)),
            dma((2,)),
            dma((2, parts)),
            dma((2,)),
            dma((2,)),
            dma((3, lines, 2)),
            dma((3, lines, 2)),
            dma((lines, len(spans))),
            dma((lines, len(spans))),
            dma((lines - 1, len(spans))),
            dma((lines - 1, len(spans))),
        ],
        compiler_params=pltpu.CompilerParams(
            collective_id=0, has_side_effects=True, vmem_limit_bytes=56 << 20
        ),
        cost_estimate=pl.CostEstimate(
            flops=6 * row_count * units * model_width,
            bytes_accessed=32 << 20,
            transcendentals=0,
        ),
        name="layer",
    )(tokens, out_grad, picks, gates, counts, weight_in, weight_out)


def local(tokens, out_grad, gates, picks, counts, w_in, w_out):
    t_dev, model_width = tokens.shape
    slot_count = picks.shape[2]
    parts = lax.axis_size("dp")
    count = lax.axis_size("expert")
    row_count = count * slot_count
    x_slices, dy_slices, all_pre, all_hidden, summed_rows, gates_grad = layer(
        tokens, out_grad, picks[0], gates[0], counts, w_in[0], w_out[0], count, parts
    )

    def weight_grad(columns, units):
        return lax.dot_general(
            columns.reshape(parts * row_count, model_width // parts),
            units.reshape(parts * row_count, units.shape[-1]),
            (((0,), (0,)), ((), ())),
            preferred_element_type=jnp.float32,
        ).astype(jnp.bfloat16)[None]

    chosen = (picks[0, 0][:, None] == jnp.arange(t_dev)[None, :]).astype(jnp.bfloat16)
    tokens_grad = lax.dot_general(
        chosen, summed_rows, (((0,), (0,)), ((), ())), preferred_element_type=jnp.float32
    ).astype(jnp.bfloat16)
    return (
        tokens_grad,
        gates_grad[None],
        weight_grad(x_slices, all_pre),
        weight_grad(dy_slices, all_hidden),
    )


def local_many(tokens, out_grad, gates, picks, counts, w_in, w_out):
    t_dev, model_width = tokens.shape
    expert_count = picks.shape[1]
    slot_count = picks.shape[2]
    part_units = w_in.shape[2]
    part_count = FF // part_units
    expert_devices = lax.axis_size("expert")
    row_index = picks[0].reshape(-1)
    live = jnp.arange(slot_count)[None, :] < counts[0][:, None]
    scale = jnp.where(live, gates[0], jnp.zeros_like(gates[0]))

    def exchange(values):
        return lax.all_to_all(values, "expert", split_axis=0, concat_axis=0, tiled=True)

    def spread(values):
        wide = jnp.broadcast_to(values[:, None], (expert_count, part_count) + values.shape[1:])
        return exchange(wide.reshape((expert_devices,) + values.shape[1:]))

    row_count = expert_devices * slot_count
    picked_shape = (expert_count, slot_count, model_width)
    rows_x = spread(tokens[row_index].reshape(picked_shape)).reshape(row_count, model_width)
    rows_dy = spread(out_grad[row_index].reshape(picked_shape)).reshape(row_count, model_width)
    row_scale = spread(scale).reshape(row_count, 1).astype(jnp.float32)
    weight_in, weight_out = w_in[0], w_out[0]
    pre = jnp.dot(rows_x, weight_in, preferred_element_type=jnp.float32)
    back = jnp.dot(rows_dy, weight_out, preferred_element_type=jnp.float32)
    hidden, gelu_back = jax.vjp(jax.nn.gelu, pre)
    gate_part = jnp.sum(hidden * back, axis=-1)
    pre_grad = gelu_back(row_scale * back)[0].astype(jnp.bfloat16)
    scaled_hidden = (row_scale * hidden).astype(jnp.bfloat16)
    row_part = lax.dot_general(
        pre_grad, weight_in, (((1,), (1,)), ((), ())), preferred_element_type=jnp.float32
    )

    def weight_grad(columns, units):
        columns = lax.all_to_all(columns, "dp", split_axis=1, concat_axis=0, tiled=True)
        units = lax.all_gather(units, "dp", axis=0, tiled=True)
        return lax.dot_general(
            columns, units, (((0,), (0,)), ((), ())), preferred_element_type=jnp.float32
        ).astype(jnp.bfloat16)[None]

    back_shape = (expert_devices, slot_count, model_width)
    back_rows = exchange(row_part.reshape(back_shape).astype(jnp.bfloat16)).astype(jnp.float32)
    back_gates = exchange(gate_part.reshape(back_shape[:2]))
    summed_rows = jnp.sum(back_rows.reshape((expert_count, part_count) + back_shape[1:]), axis=1)
    summed_gates = jnp.sum(back_gates.reshape(expert_count, part_count, slot_count), axis=1)
    empty_rows = jnp.zeros((t_dev, model_width), jnp.float32)
    tokens_grad = (
        empty_rows.at[row_index].add(summed_rows.reshape(-1, model_width)).astype(jnp.bfloat16)
    )
    gates_grad = jnp.where(live, summed_gates, jnp.zeros_like(summed_gates))[None]
    return (
        tokens_grad,
        gates_grad,
        weight_grad(rows_x, pre_grad),
        weight_grad(rows_dy, scaled_hidden),
    )


def solution(mesh):
    placed = (
        P(("expert", "dp"), None),
        P(("expert", "dp"), None),
        P(("expert", "dp"), None, None),
        P(("expert", "dp"), None, None),
        P(("expert", "dp"), None),
        P("expert", None, None),
        P("expert", None, None),
    )

    def run(*arrays):
        one = arrays[3].shape[1] == 1 and mesh.shape["dp"] == 4
        return jax.shard_map(
            local if one else local_many,
            mesh=mesh,
            in_specs=placed,
            out_specs=(
                P(("expert", "dp"), None),
                P(("expert", "dp"), None, None),
                P("expert", "dp", None),
                P("expert", "dp", None),
            ),
            check_vma=False,
        )(*arrays)

    return run
```

```python
import functools

import jax
import jax.numpy as jnp
from jax import lax
from jax.experimental import pallas as pl
from jax.experimental.pallas import tpu as pltpu
from jax.sharding import PartitionSpec as P

FF = 8192
LANES = 128
ROOT = 0.7978845608028654
CUBE = 0.044715
MESH = pl.DeviceIdType.MESH


def meet(peers):
    barrier = pltpu.get_barrier_semaphore()
    for peer in peers:
        pl.semaphore_signal(barrier, inc=1, device_id=peer, device_id_type=MESH)
    pl.semaphore_wait(barrier, len(peers))


def send(src, dst, send_sem, recv_sem, peer):
    copy = pltpu.make_async_remote_copy(
        src_ref=src,
        dst_ref=dst,
        send_sem=send_sem,
        recv_sem=recv_sem,
        device_id=peer,
        device_id_type=MESH,
    )
    copy.start()
    return copy


def layer_kernel(
    spans,
    tokens,
    out_grad,
    picks,
    gates,
    counts,
    weight_in,
    weight_out,
    slices,
    all_pre,
    all_hidden,
    rows_out,
    gates_out,
    tables,
    w1,
    w2,
    rows,
    scales,
    pre,
    back,
    gate,
    pre_grad,
    hidden,
    terms,
    beside_terms,
    pair_sum,
    line_terms,
    table_sem,
    w_sem,
    s_send,
    s_recv,
    g_send,
    g_recv,
    gx_send,
    gx_recv,
    dp_send,
    dp_recv,
    keep_sem,
    own_sem,
    a_send,
    a_recv,
    x_send,
    x_recv,
    z_send,
    z_recv,
):
    parts = all_pre.shape[0]
    count, slots, model_width = rows.shape[1:]
    row_count = count * slots
    lines = count // 2
    width = model_width // parts
    e = lax.axis_index("expert")
    d = lax.axis_index("dp")
    z = e // 2
    x = lax.rem(e, 2)
    after = lax.rem(e + 2, count)
    beside = e + 1 - 2 * x
    twin = d + 1 - 2 * lax.rem(d, 2)
    across = lax.rem(d + 2, parts)
    loads = [
        pltpu.make_async_copy(src, tables.at[i], table_sem.at[i])
        for i, src in enumerate((tokens, out_grad))
    ] + [
        pltpu.make_async_copy(src, dst, w_sem.at[i])
        for i, (src, dst) in enumerate(((weight_in, w1), (weight_out, w2)))
    ]
    for copy in loads:
        copy.start()
    group = [lax.rem(e + 2 * t, count) for t in range(1, lines)]
    group += [lax.rem(beside + 2 * t, count) for t in range(lines)]
    meet([(peer, d) for peer in group] + [(e, lax.rem(d + k, parts)) for k in range(1, parts)])
    sent = []

    def block(b, c):
        return rows.at[:, b, :, pl.ds(c * width, width)]

    def to_z(b, s, c):
        sent.append(send(block(b, c), block(b, c), g_send.at[s, c], g_recv.at[s, c], (after, d)))

    def to_beside(b, s, c):
        sent.append(send(block(b, c), block(b, c), gx_send.at[s, c], gx_recv.at[s, c], (beside, d)))

    def to_dp(b, c):
        @pl.when(d == c)
        def _():
            pltpu.make_async_copy(block(b, c), slices.at[:, d, b], keep_sem).start()

        @pl.when(d != c)
        def _():
            send(block(b, c), slices.at[:, d, b], dp_send, dp_recv.at[d], (e, c))

    def arrived(ref, sem):
        pltpu.make_async_copy(ref, ref, sem).wait()

    chosen = lax.broadcasted_iota(jnp.int32, (tables.shape[1], slots), 0) == picks[...]
    chosen = chosen.astype(jnp.float32).astype(jnp.bfloat16)
    for copy in loads[:2]:
        copy.wait()
    for c in range(parts):
        cols = slice(c * width, (c + 1) * width)
        for i in range(2):
            rows[i, e, :, cols] = lax.dot_general(
                chosen,
                tables[i, :, cols],
                (((0,), (0,)), ((), ())),
                preferred_element_type=jnp.float32,
            ).astype(jnp.bfloat16)
        to_beside(e, 0, c)
        to_z(e, 0, c)
        to_dp(e, c)
    slot = lax.broadcasted_iota(jnp.int32, (slots, slots), 1)
    live = slot == lax.broadcasted_iota(jnp.int32, (slots, slots), 0)
    live = jnp.logical_and(live, slot < counts[...])
    scale = jnp.where(live, jnp.broadcast_to(gates[...].astype(jnp.float32), (slots, slots)), 0.0)
    scale = jnp.sum(scale, axis=1, keepdims=True)
    scales[e] = jnp.broadcast_to(scale, (slots, LANES))
    for i, peer in enumerate(group):
        sent.append(send(scales.at[e], scales.at[e], s_send.at[i], s_recv.at[e], (peer, d)))

    def multiply(c):
        cols = slice(c * width, (c + 1) * width)
        for i, (weight, total) in enumerate(((w1, pre), (w2, back))):
            part = rows[i, :, :, cols].astype(jnp.float32).reshape(row_count, width)
            part = jnp.dot(
                part.astype(jnp.bfloat16), weight[cols, :], preferred_element_type=jnp.float32
            )
            if c == 0:
                total[...] = part
            else:
                total[...] += part

    for s in range(1, lines + 1):
        if s < lines:
            b = lax.rem(e + count - 2 * s, count)
            for c in range(parts):
                arrived(block(b, c), g_recv.at[s - 1, c])
                to_beside(b, s, c)
                if s < lines - 1:
                    to_z(b, s, c)
                to_dp(b, c)
        b = lax.rem(beside + count - 2 * (s - 1), count)
        for c in range(parts):
            arrived(block(b, c), gx_recv.at[s - 1, c])
            to_dp(b, c)
            if s == lines:
                if c == 0:
                    for copy in loads[2:]:
                        copy.wait()
                multiply(c)

    for peer in group:
        arrived(scales.at[peer], s_recv.at[peer])
    row_scale = scales[...].reshape(row_count, LANES)
    step = 32
    for start in range(0, row_count, step):
        here = slice(start, start + step)
        v, g, scale = pre[here, :], back[here, :], row_scale[here, :1]
        square = v * v
        bend = jnp.tanh(ROOT * v * (1.0 + CUBE * square))
        half = 0.5 * (1.0 + bend)
        value = v * half
        slope = half + 0.5 * v * (1.0 - bend * bend) * ROOT * (1.0 + 3.0 * CUBE * square)
        pre_grad[here, :] = (scale * g * slope).astype(jnp.bfloat16)
        hidden[here, :] = (scale * value).astype(jnp.bfloat16)
        gate[here, :] = jnp.broadcast_to(
            jnp.sum(value * g, axis=1, keepdims=True), (step, LANES)
        )

    pairs = ((pre_grad, all_pre), (hidden, all_hidden))
    for i, (src, dst) in enumerate(pairs):
        sent.append(send(src, dst.at[d], a_send.at[0, i], a_recv.at[0, i], (e, across)))
    for i, (src, dst) in enumerate(pairs):
        sent.append(send(src, dst.at[d], a_send.at[1, i], a_recv.at[1, i], (e, twin)))
        pltpu.make_async_copy(src, dst.at[d], own_sem.at[i]).start()

    def to_x(k, value):
        start, size = spans[k]
        cols = pl.ds(start, size)
        value = value.reshape(lines, 2, slots, size).astype(jnp.bfloat16)
        terms[0, :, :, start : start + size] = value[:, 0]
        terms[1, :, :, start : start + size] = value[:, 1]
        sent.append(
            send(
                terms.at[1 - x, :, :, cols],
                beside_terms.at[:, :, cols],
                x_send.at[k],
                x_recv.at[k],
                (beside, d),
            )
        )

    def to_lines(k):
        start, size = spans[k]
        cols = slice(start, start + size)
        here = pl.ds(start, size)
        arrived(beside_terms.at[:, :, here], x_recv.at[k])
        pair_sum[:, :, cols] = (
            terms[x, :, :, cols].astype(jnp.float32)
            + beside_terms[:, :, cols].astype(jnp.float32)
        ).astype(jnp.bfloat16)
        for t in range(1, lines):
            sent.append(
                send(
                    pair_sum.at[lax.rem(z + t, lines), :, here],
                    line_terms.at[t - 1, :, here],
                    z_send.at[t - 1, k],
                    z_recv.at[t - 1, k],
                    (lax.rem(e + 2 * t, count), d),
                )
            )

    to_x(0, gate[...])
    for k in range(1, len(spans)):
        start, size = spans[k]
        to_x(
            k,
            lax.dot_general(
                pre_grad[...],
                w1[start : start + size, :],
                (((1,), (1,)), ((), ())),
                preferred_element_type=jnp.float32,
            ),
        )
    for k in range(len(spans)):
        to_lines(k)
    for i, (_, dst) in enumerate(pairs):
        arrived(dst.at[across], a_recv.at[0, i])
        sent.append(
            send(dst.at[across], dst.at[across], a_send.at[2, i], a_recv.at[2, i], (e, twin))
        )
    for k, (start, size) in enumerate(spans):
        cols = slice(start, start + size)
        total = terms[x, z, :, cols].astype(jnp.float32)
        total += beside_terms[z, :, cols].astype(jnp.float32)
        for t in range(1, lines):
            arrived(line_terms.at[t - 1, :, pl.ds(start, size)], z_recv.at[t - 1, k])
            total += line_terms[t - 1, :, cols].astype(jnp.float32)
        if start < model_width:
            rows_out[:, cols] = total.astype(jnp.bfloat16)
        else:
            own = slot == lax.broadcasted_iota(jnp.int32, (slots, slots), 0)
            own = jnp.logical_and(own, slot < counts[...])
            total = jnp.where(own, total[:, :1], 0.0)
            gates_out[...] = jnp.sum(total, axis=0, keepdims=True)
    for i, (src, dst) in enumerate(pairs):
        pltpu.make_async_copy(src, dst.at[d], own_sem.at[i]).wait()
        for hop, owner in ((1, twin), (2, lax.rem(twin + 2, parts))):
            arrived(dst.at[owner], a_recv.at[hop, i])
    for copy in sent:
        copy.wait_send()
    arrived(slices.at[:, pl.ds(0, parts - 1)], dp_send)
    arrived(slices.at[:, d], keep_sem)
    for k in range(1, parts):
        owner = lax.rem(d + k, parts)
        arrived(slices.at[:, owner], dp_recv.at[owner])


def layer(tokens, out_grad, picks, gates, counts, weight_in, weight_out, count, parts):
    t_dev, model_width = tokens.shape
    slots = picks.shape[-1]
    units = weight_in.shape[1]
    row_count = count * slots
    lines = count // 2
    width = model_width // parts
    spans = [(model_width, LANES)] + [(k * width, width) for k in range(parts)]
    wide = model_width + LANES
    dma = pltpu.SemaphoreType.DMA
    vmem = pl.BlockSpec(memory_space=pltpu.VMEM)
    anywhere = pl.BlockSpec(memory_space=pl.ANY)
    bf16, f32 = jnp.bfloat16, jnp.float32
    return pl.pallas_call(
        functools.partial(layer_kernel, spans),
        out_shape=(
            jax.ShapeDtypeStruct((2, parts, count, slots, width), bf16),
            jax.ShapeDtypeStruct((parts, row_count, units), bf16),
            jax.ShapeDtypeStruct((parts, row_count, units), bf16),
            jax.ShapeDtypeStruct((slots, model_width), bf16),
            jax.ShapeDtypeStruct((1, slots), f32),
        ),
        in_specs=[anywhere, anywhere, vmem, vmem, vmem, anywhere, anywhere],
        out_specs=[anywhere, anywhere, anywhere, vmem, vmem],
        scratch_shapes=[
            pltpu.VMEM((2, t_dev, model_width), bf16),
            pltpu.VMEM((model_width, units), bf16),
            pltpu.VMEM((model_width, units), bf16),
            pltpu.VMEM((2, count, slots, model_width), bf16),
            pltpu.VMEM((count, slots, LANES), f32),
            pltpu.VMEM((row_count, units), f32),
            pltpu.VMEM((row_count, units), f32),
            pltpu.VMEM((row_count, LANES), f32),
            pltpu.VMEM((row_count, units), bf16),
            pltpu.VMEM((row_count, units), bf16),
            pltpu.VMEM((2, lines, slots, wide), bf16),
            pltpu.VMEM((lines, slots, wide), bf16),
            pltpu.VMEM((lines, slots, wide), bf16),
            pltpu.VMEM((lines - 1, slots, wide), bf16),
            dma((2,)),
            dma((2,)),
            dma((count - 1,)),
            dma((count,)),
            dma((lines - 1, parts)),
            dma((lines - 1, parts)),
            dma((lines, parts)),
            dma((lines, parts)),
            dma,
            dma((parts,)),
            dma,
            dma((2,)),
            dma((3, 2)),
            dma((3, 2)),
            dma((len(spans),)),
            dma((len(spans),)),
            dma((lines - 1, len(spans))),
            dma((lines - 1, len(spans))),
        ],
        compiler_params=pltpu.CompilerParams(
            collective_id=0, has_side_effects=True, vmem_limit_bytes=56 << 20
        ),
        cost_estimate=pl.CostEstimate(
            flops=6 * row_count * units * model_width,
            bytes_accessed=32 << 20,
            transcendentals=0,
        ),
        name="layer",
    )(tokens, out_grad, picks, gates, counts, weight_in, weight_out)


def local(tokens, out_grad, gates, picks, counts, w_in, w_out):
    t_dev, model_width = tokens.shape
    slot_count = picks.shape[2]
    parts = lax.axis_size("dp")
    count = lax.axis_size("expert")
    row_count = count * slot_count
    slices, all_pre, all_hidden, summed_rows, gates_grad = layer(
        tokens, out_grad, picks[0], gates[0], counts, w_in[0], w_out[0], count, parts
    )

    def weight_grad(columns, units):
        return lax.dot_general(
            columns.reshape(parts * row_count, model_width // parts),
            units.reshape(parts * row_count, units.shape[-1]),
            (((0,), (0,)), ((), ())),
            preferred_element_type=jnp.float32,
        ).astype(jnp.bfloat16)[None]

    chosen = (picks[0, 0][:, None] == jnp.arange(t_dev)[None, :]).astype(jnp.bfloat16)
    tokens_grad = lax.dot_general(
        chosen, summed_rows, (((0,), (0,)), ((), ())), preferred_element_type=jnp.float32
    ).astype(jnp.bfloat16)
    return (
        tokens_grad,
        gates_grad[None],
        weight_grad(slices[0], all_pre),
        weight_grad(slices[1], all_hidden),
    )


def local_many(tokens, out_grad, gates, picks, counts, w_in, w_out):
    t_dev, model_width = tokens.shape
    expert_count = picks.shape[1]
    slot_count = picks.shape[2]
    part_units = w_in.shape[2]
    part_count = FF // part_units
    expert_devices = lax.axis_size("expert")
    row_index = picks[0].reshape(-1)
    live = jnp.arange(slot_count)[None, :] < counts[0][:, None]
    scale = jnp.where(live, gates[0], jnp.zeros_like(gates[0]))

    def exchange(values):
        return lax.all_to_all(values, "expert", split_axis=0, concat_axis=0, tiled=True)

    def spread(values):
        wide = jnp.broadcast_to(values[:, None], (expert_count, part_count) + values.shape[1:])
        return exchange(wide.reshape((expert_devices,) + values.shape[1:]))

    row_count = expert_devices * slot_count
    picked_shape = (expert_count, slot_count, model_width)
    rows_x = spread(tokens[row_index].reshape(picked_shape)).reshape(row_count, model_width)
    rows_dy = spread(out_grad[row_index].reshape(picked_shape)).reshape(row_count, model_width)
    row_scale = spread(scale).reshape(row_count, 1).astype(jnp.float32)
    weight_in, weight_out = w_in[0], w_out[0]
    pre = jnp.dot(rows_x, weight_in, preferred_element_type=jnp.float32)
    back = jnp.dot(rows_dy, weight_out, preferred_element_type=jnp.float32)
    hidden, gelu_back = jax.vjp(jax.nn.gelu, pre)
    gate_part = jnp.sum(hidden * back, axis=-1)
    pre_grad = gelu_back(row_scale * back)[0].astype(jnp.bfloat16)
    scaled_hidden = (row_scale * hidden).astype(jnp.bfloat16)
    row_part = lax.dot_general(
        pre_grad, weight_in, (((1,), (1,)), ((), ())), preferred_element_type=jnp.float32
    )

    def weight_grad(columns, units):
        columns = lax.all_to_all(columns, "dp", split_axis=1, concat_axis=0, tiled=True)
        units = lax.all_gather(units, "dp", axis=0, tiled=True)
        return lax.dot_general(
            columns, units, (((0,), (0,)), ((), ())), preferred_element_type=jnp.float32
        ).astype(jnp.bfloat16)[None]

    back_shape = (expert_devices, slot_count, model_width)
    back_rows = exchange(row_part.reshape(back_shape).astype(jnp.bfloat16)).astype(jnp.float32)
    back_gates = exchange(gate_part.reshape(back_shape[:2]))
    summed_rows = jnp.sum(back_rows.reshape((expert_count, part_count) + back_shape[1:]), axis=1)
    summed_gates = jnp.sum(back_gates.reshape(expert_count, part_count, slot_count), axis=1)
    empty_rows = jnp.zeros((t_dev, model_width), jnp.float32)
    tokens_grad = (
        empty_rows.at[row_index].add(summed_rows.reshape(-1, model_width)).astype(jnp.bfloat16)
    )
    gates_grad = jnp.where(live, summed_gates, jnp.zeros_like(summed_gates))[None]
    return (
        tokens_grad,
        gates_grad,
        weight_grad(rows_x, pre_grad),
        weight_grad(rows_dy, scaled_hidden),
    )


def solution(mesh):
    placed = (
        P(("expert", "dp"), None),
        P(("expert", "dp"), None),
        P(("expert", "dp"), None, None),
        P(("expert", "dp"), None, None),
        P(("expert", "dp"), None),
        P("expert", None, None),
        P("expert", None, None),
    )

    def run(*arrays):
        one = arrays[3].shape[1] == 1 and mesh.shape["dp"] == 4
        return jax.shard_map(
            local if one else local_many,
            mesh=mesh,
            in_specs=placed,
            out_specs=(
                P(("expert", "dp"), None),
                P(("expert", "dp"), None, None),
                P("expert", "dp", None),
                P("expert", "dp", None),
            ),
            check_vma=False,
        )(*arrays)

    return run
```
